256 devices in a mesh: expert: 32 (over x, y, core), seq: 8 (over z).
Axes of the slice: x: 4, y: 4, z: 8, core: 2. Of those that a mesh axis runs over, the one named last changes fastest.
Arguments:
- resid: bfloat16 [65536, 2048], P(('expert', 'seq')), may hold values from -6 to 6
- gate_in: bfloat16 [65536, 2048], P(('expert', 'seq')), may hold values from -6 to 6
- gate_short: float32 [3, 2048], replicated, may hold values from -3 to 3
- value_short: float32 [3, 2048], replicated, may hold values from -3 to 3
- long_filter: bfloat16 [4096, 2048], P('expert', 'seq'), may hold values from -2 to 2
- skip_gain: float32 [2048], P('seq'), may hold values from -3 to 3
- norm_gain: float32 [2048], replicated, may hold values from 0.5 to 1.5
- expert_ids: int32 [65536, 4], P(('expert', 'seq')), may hold values from 0 to 63, all different within a row; in each aligned block of 256 rows (0 to 255, 256 to 511, ...) at most 24 rows name the same one
- gate_wts: float32 [65536, 4], P(('expert', 'seq')), may hold values from 0.05 to 0.6
- spare_pick: int32 [32], replicated, may hold values from 0 to 1
- w_gate: bfloat16 [64, 2048, 256], P('expert'), may hold values from -0.125 to 0.125
- w_up: bfloat16 [64, 2048, 256], P('expert'), may hold values from -0.125 to 0.125
- w_down: bfloat16 [64, 2048, 256], P('expert'), may hold values from -0.375 to 0.375
Outputs:
- mixed: bfloat16 [65536, 2048], P(('expert', 'seq'))
The draws below stay inside these ranges and needn't reach their ends.
Inputs may be any that keep to these rules, and one draw needn't show every extreme that they name: `expert_ids`: in each aligned block of 256 tokens no expert is named by more than 24 entries, and some expert by exactly that many; each token names 4 different experts.
All inputs are finite; a program needn't handle non-finite values.
Results may differ from the reference program's by a relative error of at most 0.0051.
Values may be sent and summed in bfloat16 or wider, within the bound.
A program may use at most 128 MiB of HBM per device.

```python
import math
import jax
import jax.numpy as jnp
import numpy as np
from jax import lax

D = 2048
H = 256
EXP_DEV = 2
TOPK = 4
LEN_DEV = 256
SEQ_LEN = 4096
SEQS = 16
TOKENS = 65536
EXPERTS = 64
CAP = 12
N_EXPERT = 32


def draw_long_filter(key, part):
    key = jax.random.fold_in(key, 7)
    rate_key, noise_key = jax.random.split(key)
    rate = jnp.exp(jax.random.uniform(rate_key, (D,), jnp.float32, jnp.log(0.5 / SEQ_LEN), jnp.log(0.05)))
    steps = jnp.arange(SEQ_LEN, dtype=jnp.float32)[:, None]
    noise = jax.random.normal(noise_key, (SEQ_LEN, D), jnp.float32)
    values = noise * jnp.exp(-rate[None, :] * steps) * jnp.sqrt(2.0 * rate)[None, :]
    return jnp.clip(values, -2.0, 2.0).astype(jnp.bfloat16)


def plant(values, rng, least, high):
    index_at = [jax.random.randint(jax.random.fold_in(rng, axis), (), 0, length) for axis, length in enumerate(values.shape)]
    longest = values.shape.index(max(values.shape))
    neighbour = index_at[:longest] + [(index_at[longest] + 1) % values.shape[longest]] + index_at[longest + 1:]
    return values.at[tuple(index_at)].set(least).at[tuple(neighbour)].set(high)


def block_levels(stream_key, dims, cuts, least, largest):
    def one(dim, shards_of):
        draws = jax.random.uniform(jax.random.fold_in(jax.random.fold_in(stream_key, 6), dim), (shards_of,), jnp.float32, least / len(cuts), largest / len(cuts))
        return jnp.repeat(jnp.exp(draws), dims[dim] // shards_of).reshape((-1,) + (1,) * (len(dims) - dim - 1))

    level = one(*cuts[0])
    for cut in cuts[1:]:
        level = level * one(*cut)
    return level


def shared_out(key, own, number, rows, amount, top, limit, lean):
    ranking = jax.random.permutation(key, amount)
    packed, common = shares(amount, rows * top, limit, lean, True), shares(amount, rows * top, limit, lean, False)
    places = jnp.arange(amount)

    def named(lengths, rotation):
        used = int((lengths > 0).sum())
        fixed = max(1, used // 4)
        moved = fixed + (places - fixed + rotation * (used - fixed)) % max(1, amount - fixed)
        return jnp.zeros((amount,), jnp.int32).at[ranking[jnp.where(places < fixed, places, moved)]].set(jnp.asarray(lengths, jnp.int32))

    lengths = jnp.where(number % 4 == 0, named(packed, number // 4), named(common, number - number // 4 - 1))
    mixed = jax.random.permutation(jax.random.fold_in(own, 3), amount)
    source_of, receiver = mixed[0:amount // 2 * 2:2], mixed[1:amount // 2 * 2:2]
    room = jnp.minimum(lengths[source_of] - 1, limit - lengths[receiver]) // 2
    room = jnp.where((source_of == ranking[0]) | (receiver == ranking[0]) | (lengths[receiver] == 0), 0, jnp.maximum(room, 0))
    moved = jax.random.randint(jax.random.fold_in(own, 4), (amount // 2,), 0, 1 << 20) % (room + 1)
    lengths = lengths.at[source_of].add(-moved).at[receiver].add(moved)
    members = jnp.searchsorted(jnp.cumsum(lengths), jnp.arange(rows * top), side="right").astype(jnp.int32)
    grid = members.reshape(top, rows).T
    grid = grid[jax.random.permutation(jax.random.fold_in(own, 1), rows)]
    rotation = jax.random.randint(jax.random.fold_in(own, 2), (rows, 1), 0, top)
    return jnp.take_along_axis(grid, (jnp.arange(top)[None, :] + rotation) % top, axis=1)


def shares(amount, total, most, skew, full):
    portions = [(1 << 20) // math.isqrt(grade ** skew) + 1 for grade in range(1, amount + 1)]
    largest = most if full else min(most, max(-(-total // amount), total * portions[0] // sum(portions)))
    least = 1 if total - largest >= amount - 1 else 0
    holding, rest = [largest] + [least] * (amount - 1), total - largest - least * (amount - 1)
    while rest > 0:
        candidates = [i for i in range(1, amount) if holding[i] < largest] or [i for i in range(1, amount) if holding[i] < most]
        pool, left = sum([portions[i] for i in candidates]), rest
        for i in candidates:
            more = min(most - holding[i], max(1, left * portions[i] // pool), rest)
            holding[i] = holding[i] + more
            rest = rest - more
    return np.array(holding)


def bell_draw(rng, dims, spread, reach, shards=(), kind=jnp.bfloat16):
    array = jax.random.normal(rng, dims, jnp.float32) * spread
    if len(shards) > 0:
        array = block_levels(rng, dims, shards, -0.22, 0.18) * array
    return jnp.clip(array, min=-reach, max=reach).astype(kind)


def setup_inputs(seed: int = 0) -> dict:
    streams_of = jax.random.split(jax.random.key(seed), 14)
    resid = bell_draw(streams_of[0], (TOKENS, D), 1.0, 6.0, ((0, 256),))
    gate_in = bell_draw(streams_of[1], (TOKENS, D), 1.0, 6.0, ((0, 256),))
    gate_short = bell_draw(streams_of[2], (3, D), 0.5, 3.0, (), jnp.float32)
    value_short = bell_draw(streams_of[3], (3, D), 0.5, 3.0, (), jnp.float32)
    long_filter = draw_long_filter(jax.random.fold_in(streams_of[13], 71), 0)
    skip_gain = bell_draw(streams_of[5], (D,), 0.5, 3.0, ((0, 8),), jnp.float32)
    norm_gain = jnp.clip(1.0 + 0.1 * jax.random.normal(streams_of[6], (D,), jnp.float32), 0.5, 1.5)
    expert_ids_keys = jax.random.split(jax.random.fold_in(streams_of[7], 1), TOKENS // LEN_DEV)
    expert_ids_turns = jax.random.permutation(jax.random.fold_in(streams_of[7], 3), TOKENS // LEN_DEV)
    expert_ids = jax.vmap(lambda own, number: shared_out(jax.random.fold_in(streams_of[7], 2), own, number, LEN_DEV, EXPERTS, TOPK, 2 * CAP, 2))(expert_ids_keys, expert_ids_turns).reshape((TOKENS, TOPK))
    gate_wts = jnp.clip(jnp.exp(math.log(0.6) - 2.4849067 * jax.random.uniform(streams_of[8], (TOKENS, TOPK), jnp.float32) ** block_levels(streams_of[8], (TOKENS, TOPK), ((0, 256),), -0.2, 0.2)), 0.05, 0.6)
    spare_pick = plant(jax.random.randint(streams_of[9], (N_EXPERT,), 0, EXP_DEV), jax.random.fold_in(streams_of[9], 1), 0, EXP_DEV - 1).astype(jnp.int32)
    w_gate = bell_draw(streams_of[10], (EXPERTS, D, H), D ** -0.5, 0.125, ((0, 32),))
    w_up = bell_draw(streams_of[11], (EXPERTS, D, H), D ** -0.5, 0.125, ((0, 32),))
    w_down = bell_draw(streams_of[12], (EXPERTS, D, H), H ** -0.5, 0.375, ((0, 32),))
    return {"resid": resid, "gate_in": gate_in, "gate_short": gate_short, "value_short": value_short, "long_filter": long_filter, "skip_gain": skip_gain, "norm_gain": norm_gain, "expert_ids": expert_ids, "gate_wts": gate_wts, "spare_pick": spare_pick, "w_gate": w_gate, "w_up": w_up, "w_down": w_down}


def short_conv(signal, kernel):
    widened = signal.astype(jnp.float32)
    padded = jnp.pad(widened, ((0, 0), (2, 0), (0, 0)))
    return kernel[0] * widened + kernel[1] * padded[:, 1:-1] + kernel[2] * padded[:, :-2]

def reference(resid, gate_in, gate_short, value_short, long_filter, skip_gain, norm_gain, expert_ids, gate_wts, spare_pick, w_gate, w_up, w_down):
    seq_resid = resid.reshape(SEQS, SEQ_LEN, D)
    gated = short_conv(gate_in.reshape(SEQS, SEQ_LEN, D), gate_short)
    values = short_conv(seq_resid, value_short).astype(jnp.bfloat16)
    fft_len = 2 * SEQ_LEN
    filt_freq = jnp.fft.rfft(long_filter.astype(jnp.float32), n=fft_len, axis=0)

    def one_sequence(seq_values):
        widened = seq_values.astype(jnp.float32)
        spectrum = jnp.fft.rfft(widened, n=fft_len, axis=0) * filt_freq
        conv = jnp.fft.irfft(spectrum, n=fft_len, axis=0)[:SEQ_LEN]
        return (conv + skip_gain * widened).astype(jnp.bfloat16)
    longconv = lax.map(one_sequence, values)
    hidden = (seq_resid.astype(jnp.float32) + gated * longconv.astype(jnp.float32)).reshape(TOKENS, D)
    scale = lax.rsqrt(lax.optimization_barrier(jnp.mean(hidden * hidden, axis=-1, keepdims=True)) + 1e-05)
    normed = (hidden * scale * norm_gain).astype(jnp.bfloat16)
    tile_rows = 256
    tokens = TOKENS
    entries = tokens * TOPK
    flat_x = normed
    blocks = expert_ids.reshape(tokens // LEN_DEV, LEN_DEV * TOPK)
    onehot = (blocks[:, :, None] == jnp.arange(EXPERTS, dtype=jnp.int32)[None, None, :]).astype(jnp.int32)
    rank = lax.optimization_barrier(jnp.sum((jnp.cumsum(onehot, axis=1) - onehot) * onehot, axis=2)).reshape(entries)
    ids = blocks.reshape(entries)
    home = ids // EXP_DEV
    local = ids % EXP_DEV
    partner = (home + N_EXPERT // 2) % N_EXPERT
    replicated = spare_pick[partner] == local
    kept = (rank < CAP) | (rank < 2 * CAP) & replicated
    sort_key = jnp.where(kept, ids, EXPERTS).astype(jnp.int32)
    counts = jax.ops.segment_sum(jnp.ones((entries,), jnp.int32), sort_key, num_segments=EXPERTS + 1)[:EXPERTS]
    order = jnp.argsort(sort_key, stable=True).astype(jnp.int32)
    sorted_key = sort_key[order]
    padded = (counts + tile_rows - 1) // tile_rows * tile_rows
    pad_start = jnp.cumsum(padded) - padded
    count_start = jnp.cumsum(counts) - counts
    rows_total = entries + EXPERTS * tile_rows
    safe_key = jnp.minimum(sorted_key, EXPERTS - 1)
    position = jnp.arange(entries, dtype=jnp.int32)
    dest = jnp.where(sorted_key < EXPERTS, pad_start[safe_key] + position - count_start[safe_key], rows_total)
    row_tok = jnp.zeros((rows_total,), jnp.int32).at[dest].set(order // TOPK, mode='drop')
    row_wts = jnp.zeros((rows_total,), jnp.float32).at[dest].set(gate_wts.reshape(entries)[order], mode='drop')
    n_tiles = rows_total // tile_rows
    tile_start = jnp.arange(n_tiles, dtype=jnp.int32) * tile_rows
    tile_expert = jnp.minimum(lax.optimization_barrier(jnp.sum(((pad_start + padded)[None, :] <= tile_start[:, None]).astype(jnp.int32), axis=1)), EXPERTS - 1)

    def one_tile(total, index):
        expert = tile_expert[index]
        toks = lax.dynamic_slice_in_dim(row_tok, index * tile_rows, tile_rows)
        wts = lax.dynamic_slice_in_dim(row_wts, index * tile_rows, tile_rows)
        rows = flat_x[toks]
        gate = jnp.dot(rows, w_gate[expert], preferred_element_type=jnp.float32)
        upper = jnp.dot(rows, w_up[expert], preferred_element_type=jnp.float32)
        act = (jax.nn.silu(gate) * upper).astype(jnp.bfloat16)
        out = lax.dot_general(act, w_down[expert], (((1,), (1,)), ((), ())), preferred_element_type=jnp.float32).astype(jnp.bfloat16)
        out = lax.optimization_barrier(out).astype(jnp.float32)
        return (total.at[toks].add(wts[:, None] * out), None)
    moe, _ = lax.scan(one_tile, jnp.zeros((tokens, D), jnp.float32), jnp.arange(n_tiles, dtype=jnp.int32))
    return (hidden + moe).astype(jnp.bfloat16)
```

```python
import functools

import jax
import jax.numpy as jnp
from jax import lax
from jax.experimental import pallas as pl
from jax.experimental.pallas import tpu as pltpu
from jax.sharding import PartitionSpec as P

F32, BF16, I32 = jnp.float32, jnp.bfloat16, jnp.int32
VMEM_LIMIT = 56 * 1024 * 1024
TOK = 256
WIDTH = 2048
HOMES = 32
GROUPS = 8
SEQS = 16
BLOCKS = 16
CH = 8
POS = SEQS * TOK
QUARTERS = 4
QW = WIDTH // QUARTERS
MAIN = 32
LEFT = 4
MSG = QUARTERS * (MAIN + LEFT)
CAP = 12
HID = 256
PAD = 128


def iota(shape, dim):
    return lax.broadcasted_iota(I32, shape, dim)


def eye(n):
    return (iota((n, n), 0) == iota((n, n), 1)).astype(BF16)


def nt(a, b):
    return lax.dot_general(a, b, (((1,), (1,)), ((), ())), preferred_element_type=F32)


def mm(a, b):
    return jnp.dot(a, b, preferred_element_type=F32)


def short_conv(x, before2, before1, kernel):
    row = iota(x.shape, 0)
    back1 = jnp.where(row == 0, before1, pltpu.roll(x, 1, 0))
    back2 = jnp.where(row == 0, before2, jnp.where(row == 1, before1, pltpu.roll(x, 2, 0)))
    return kernel[0:1] * x + kernel[1:2] * back1 + kernel[2:3] * back2


def group_cols(g):
    return pl.ds(pl.multiple_of(g * 256, 256), 256)


def to_message(block):
    first = block[:, :128].reshape(32, 8, 128)
    second = block[:, 128:].reshape(32, 8, 128)
    return jnp.concatenate([first, second], axis=1).astype(BF16)


def from_message(message):
    wide = message.astype(F32)
    first = wide[:, :8].reshape(256, 128).astype(BF16)
    second = wide[:, 8:].reshape(256, 128).astype(BF16)
    ident = eye(128)
    return jnp.concatenate([nt(ident, first), nt(ident, second)], axis=0)


def values_kernel(resid_ref, rim_ref, kern_ref, filt_ref, out_ref, filt_out_ref):
    ident = eye(256)

    def one(g, _):
        cols = group_cols(g)
        x = resid_ref[:, cols].astype(F32)
        values = short_conv(x, rim_ref[2:3, cols], rim_ref[3:4, cols], kern_ref[:, cols]).astype(BF16)
        out_ref[:, g] = to_message(nt(ident, values))
        return 0

    lax.fori_loop(0, GROUPS, one, 0)
    filt_out_ref[...] = nt(ident, filt_ref[...]).reshape(HOMES, CH, 128)


def build_bank(row, bank_ref):
    wide = jnp.concatenate([jnp.broadcast_to(row, (8, POS)), jnp.zeros((8, PAD), F32)], axis=1)
    base = pltpu.roll(wide, 0, 1, stride=1, stride_axis=0)
    for a in range(8):
        upper = pltpu.roll(base, 16 * a, 1) if a else base
        lower = pltpu.roll(base, 16 * a + 8, 1)
        both = jnp.concatenate([upper, lower], axis=0)[:, :POS].astype(BF16)
        bank_ref[16 * a : 16 * a + 16, :] = both
        bank_ref[128 + 16 * a : 144 + 16 * a, PAD:] = both[:, : POS - PAD]


def conv_kernel(recv_ref, filt_ref, skip_ref, out_ref, wide_ref, hrow_ref, x_ref, y_ref, bank_ref, acc_ref):
    for e in range(HOMES):
        hrow_ref[:, 128 * e : 128 * e + 128] = filt_ref[e]
    bank_ref[128:, :PAD] = jnp.zeros((128, PAD), BF16)
    for i in range(BLOCKS):
        wide_ref[i * 256 : i * 256 + 256] = recv_ref[:, i].astype(F32).reshape(256, 128)
    for c in range(CH):
        for half in range(2):
            x_ref[c, :, 128 * half : 128 * half + 128] = wide_ref[pl.ds(8 * half + c, 256, stride=16), :]

    def one(c, _):
        build_bank(hrow_ref[pl.ds(c, 1), :], bank_ref)
        x = x_ref[c]
        lhs = x.astype(BF16)
        acc_ref[...] = x * skip_ref[pl.ds(c, 1), :]
        for k in range(BLOCKS):
            acc_ref[16 * k :, :] += mm(lhs[: 256 - 16 * k], bank_ref[:, 256 * k : 256 * k + 256])
        y_ref[c] = acc_ref[...]
        return 0

    lax.fori_loop(0, CH, one, 0)
    for c in range(CH):
        for half in range(2):
            wide_ref[pl.ds(8 * half + c, 256, stride=16), :] = y_ref[c, :, 128 * half : 128 * half + 128]
    for i in range(BLOCKS):
        out_ref[:, i] = wide_ref[i * 256 : i * 256 + 256].reshape(SEQS, 16, 128).astype(BF16)


def slots(named, rep, axis):
    tri = (iota((TOK, TOK), axis) < iota((TOK, TOK), 1 - axis)).astype(BF16)
    if axis == 0:
        rank = mm(named.astype(BF16), tri)
    else:
        rank = mm(tri, named.astype(BF16))
    kept = (named > 0) & ((rank < CAP) | ((rank < 2 * CAP) & (rep > 0)))
    return jnp.where(kept, jnp.where(rep > 0, rank, rank + 2 * CAP), -1.0)


def norm_kernel(
    back_ref, resid_ref, gate_in_ref, rim_ref, kern_ref, gain_ref, idst_ref, rep_ref, send_ref, hid_ref, normed_ref, slot_ref
):
    hid_ref, send_ref = hid_ref, send_ref

    def one(g, total):
        cols = group_cols(g)
        x = gate_in_ref[:, cols].astype(F32)
        gated = short_conv(x, rim_ref[0:1, cols], rim_ref[1:2, cols], kern_ref[:, cols])
        hidden = resid_ref[:, cols].astype(F32) + gated * from_message(back_ref[:, g])
        hid_ref[:, cols] = hidden
        return total + jnp.sum(hidden * hidden, axis=1, keepdims=True)

    total = lax.fori_loop(0, GROUPS, one, jnp.zeros((TOK, 1), F32))
    scale = lax.rsqrt(total * (1.0 / WIDTH) + 1e-05)

    def two(g, _):
        cols = group_cols(g)
        normed_ref[:, cols] = (hid_ref[:, cols] * scale * gain_ref[:, cols]).astype(BF16)
        return 0

    lax.fori_loop(0, GROUPS, two, 0)
    named = jnp.zeros((64, TOK), F32)
    for k in range(4):
        named += (idst_ref[k : k + 1, :] == iota((64, TOK), 0)).astype(F32)
    slot_ref[...] = slots(named, rep_ref[...], 0)

    def four(h, _):
        rows = MAIN * 8
        sel = []
        left = []
        for j in range(8):
            even = slot_ref[pl.ds(16 * h + 2 * j, 1), :]
            odd = slot_ref[pl.ds(16 * h + 2 * j + 1, 1), :]
            r = iota((MAIN, TOK), 0).astype(F32)
            sel.append(((even == r) | (odd == r)).astype(BF16))
            r = (iota((16, TOK), 0) % 4 + MAIN).astype(F32)
            left.append(((even == r) | (odd == r)).astype(F32))
        sel = jnp.concatenate(sel, axis=0)
        left = jnp.concatenate(left, axis=0)
        part = iota((128, TOK), 0) % 16 // 4
        spill = jnp.zeros((128, QW), F32)
        for q in range(QUARTERS):
            cols = normed_ref[:, QW * q : QW * q + QW]
            send_ref[pl.ds(8 * h, 8), MAIN * q : MAIN * q + MAIN, :] = mm(sel, cols).astype(BF16).reshape(8, MAIN, QW)
            spill += mm(jnp.where(part == q, left, 0.0).astype(BF16), cols)
        send_ref[pl.ds(8 * h, 8), MAIN * QUARTERS :, :] = spill.astype(BF16).reshape(8, 16, QW)
        return 0

    lax.fori_loop(0, HOMES // 8, four, 0)


def silu_mul(gate, up):
    return gate / (1.0 + jnp.exp(-gate)) * up


def ffn_group(first, n, recv_ref, wg_ref, wu_ref, wd_ref, out_ref, hot):
    cold = 1 - hot
    src = pl.ds(first, n)
    rows = 16 * n
    zero = functools.partial(jnp.zeros, (rows, HID), F32)
    ga, ua, gb, ub, gc, uc, gl, ul = (zero() for _ in range(8))
    left = recv_ref[src, MAIN * QUARTERS :, :].reshape(rows, QW)
    part = iota((rows, HID), 0) % 16 // 4
    for q in range(QUARTERS):
        xa = recv_ref[src, MAIN * q : MAIN * q + 16, :].reshape(rows, QW)
        xb = recv_ref[src, MAIN * q + 16 : MAIN * q + 32, :].reshape(rows, QW)
        cut = slice(QW * q, QW * q + QW)
        both = jnp.concatenate([xa, xb], axis=0)
        gh, uh = mm(both, wg_ref[hot, cut, :]), mm(both, wu_ref[hot, cut, :])
        ga, ua, gb, ub = ga + gh[:rows], ua + uh[:rows], gb + gh[rows:], ub + uh[rows:]
        both = jnp.concatenate([xb, left], axis=0)
        gh, uh = mm(both, wg_ref[cold, cut, :]), mm(both, wu_ref[cold, cut, :])
        gc, uc = gc + gh[:rows], uc + uh[:rows]
        gl = gl + jnp.where(part == q, gh[rows:], 0.0)
        ul = ul + jnp.where(part == q, uh[rows:], 0.0)

    def over_quarters(acc):
        acc = acc.reshape(n, 16, HID)
        acc = acc[:, :8] + acc[:, 8:]
        acc = acc.reshape(8 * n, HID)
        low = iota(acc.shape, 0) % 8 < 4
        other = jnp.where(low, pltpu.roll(acc, 8 * n - 4, 0), pltpu.roll(acc, 4, 0))
        acc = (acc + other).reshape(n, 8, HID)
        return jnp.concatenate([acc, acc], axis=1).reshape(rows, HID)

    is_hot = iota((rows, HID), 0) % 16 < 8
    act_a = silu_mul(ga, ua).astype(BF16)
    act_b = silu_mul(jnp.where(is_hot, gb, gc), jnp.where(is_hot, ub, uc))
    act_bh = jnp.where(is_hot, act_b, 0.0).astype(BF16)
    act_bc = jnp.where(is_hot, 0.0, act_b).astype(BF16)
    act_l = silu_mul(over_quarters(gl), over_quarters(ul)).astype(BF16)
    hot_in = jnp.concatenate([act_a, act_bh], axis=0)
    cold_in = jnp.concatenate([act_bc, act_l], axis=0)
    part = iota((rows, QW), 0) % 16 // 4
    spill = jnp.zeros((rows, QW), F32)
    for q in range(QUARTERS):
        cut = slice(QW * q, QW * q + QW)
        oh = nt(hot_in, wd_ref[hot, cut, :])
        oc = nt(cold_in, wd_ref[cold, cut, :])
        out_ref[src, MAIN * q : MAIN * q + 16, :] = oh[:rows].astype(BF16).reshape(n, 16, QW)
        out_ref[src, MAIN * q + 16 : MAIN * q + 32, :] = (oh[rows:] + oc[:rows]).astype(BF16).reshape(n, 16, QW)
        spill = jnp.where(part == q, oc[rows:], spill)
    out_ref[src, MAIN * QUARTERS :, :] = spill.astype(BF16).reshape(n, 16, QW)


def ffn_kernel(hot_ref, recv_ref, wg_ref, wu_ref, wd_ref, out_ref):
    hot = hot_ref[0]

    def one(i, _):
        ffn_group(16 * i, 16, recv_ref, wg_ref, wu_ref, wd_ref, out_ref, hot)
        return 0

    lax.fori_loop(0, HOMES // 16, one, 0)


def combine_weights(ids_ref, wts_ref, rep_ref, wmain_ref, wleft_ref):
    named = jnp.zeros((TOK, 64), F32)
    weight = jnp.zeros((TOK, 64), F32)
    for k in range(4):
        hit = ids_ref[:, k : k + 1] == iota((TOK, 64), 1)
        named += hit.astype(F32)
        weight += jnp.where(hit, wts_ref[:, k : k + 1], 0.0)
    slot = slots(named, rep_ref[...], 1).astype(BF16)
    whi = weight.astype(BF16)
    wlo = (weight - whi.astype(F32)).astype(BF16)

    def spread(per, want, block):
        lanes = HOMES * per // 4
        lane = iota((64, lanes), 1) + block * lanes
        expert = iota((64, lanes), 0)
        high = low = jnp.zeros((TOK, lanes), F32)
        for odd in range(2):
            pick = (expert == 2 * (lane // per) + odd).astype(BF16)
            hit = mm(slot, pick) == want
            high = high + jnp.where(hit, mm(whi, pick), 0.0)
            low = low + jnp.where(hit, mm(wlo, pick), 0.0)
        return high.astype(BF16), low.astype(BF16)

    for block in range(4):
        want = (iota((TOK, 8 * MAIN), 1) % MAIN).astype(F32)
        high, low = spread(MAIN, want, block)
        wmain_ref[0, :, 256 * block : 256 * block + 256] = high
        wmain_ref[1, :, 256 * block : 256 * block + 256] = low
        want = (iota((TOK, 8 * 16), 1) % 4 + MAIN).astype(F32)
        high, low = spread(16, want, block)
        wleft_ref[0, :, 128 * block : 128 * block + 128] = high
        wleft_ref[1, :, 128 * block : 128 * block + 128] = low


def combine_kernel(ret_ref, hid_ref, ids_ref, wts_ref, rep_ref, out_ref, wmain_ref, wleft_ref):
    combine_weights(ids_ref, wts_ref, rep_ref, wmain_ref, wleft_ref)
    left = ret_ref[:, MAIN * QUARTERS :, :].reshape(HOMES * 16, QW)
    part = iota((TOK, HOMES * 16), 1) % 16 // 4
    for q in range(QUARTERS):
        main = ret_ref[:, MAIN * q : MAIN * q + MAIN, :].reshape(HOMES * MAIN, QW)
        moe = mm(wmain_ref[0], main) + mm(wmain_ref[1], main)
        for w in range(2):
            moe += mm(jnp.where(part == q, wleft_ref[w].astype(F32), 0.0).astype(BF16), left)
        cut = slice(QW * q, QW * q + QW)
        out_ref[:, cut] = (hid_ref[:, cut] + moe).astype(BF16)


def whole(n):
    return [pl.BlockSpec(memory_space=pltpu.VMEM)] * n


def call(kernel, outs, scratch, *args, smem=0):
    return pl.pallas_call(
        kernel,
        out_shape=outs,
        in_specs=[pl.BlockSpec(memory_space=pltpu.SMEM)] * smem + whole(len(args) - smem),
        out_specs=whole(1)[0] if not isinstance(outs, tuple) else tuple(whole(len(outs))),
        scratch_shapes=scratch,
        compiler_params=pltpu.CompilerParams(vmem_limit_bytes=VMEM_LIMIT),
    )(*args)


def body(
    resid,
    gate_in,
    gate_short,
    value_short,
    long_filter,
    skip_gain,
    norm_gain,
    expert_ids,
    gate_wts,
    spare_pick,
    w_gate,
    w_up,
    w_down,
):
    n_seq = lax.axis_size("seq")
    n_exp = lax.axis_size("expert")
    me = lax.axis_index("expert")
    z = lax.axis_index("seq")
    tails = jnp.stack([gate_in[-2:], resid[-2:]])
    count = n_exp * n_seq
    rims = lax.ppermute(tails, ("expert", "seq"), [(i, i + 1) for i in range(count - 1)])
    rims = jnp.where((z == 0) & (me % 2 == 0), jnp.zeros((), BF16), rims)
    rims = rims.astype(F32).reshape(4, WIDTH)
    sds = jax.ShapeDtypeStruct
    values, filt = call(
        values_kernel,
        (sds((HOMES, GROUPS, 16, 128), BF16), sds((HOMES, CH, 128), F32)),
        [],
        resid,
        rims,
        value_short,
        long_filter,
    )
    both = ("expert", "seq")
    values = lax.all_to_all(values.reshape(256, 16, 128), both, split_axis=0, concat_axis=0, tiled=True)
    filt = lax.all_to_all(filt, "expert", split_axis=0, concat_axis=0, tiled=True)
    skip = lax.dynamic_slice_in_dim(skip_gain, me * CH, CH, 0)
    skip = jnp.broadcast_to(skip[:, None], (CH, 256))
    conv = call(
        conv_kernel,
        sds((SEQS, BLOCKS, 16, 128), BF16),
        [
            pltpu.VMEM((POS, 128), F32),
            pltpu.VMEM((CH, POS), F32),
            pltpu.VMEM((CH, 256, 256), F32),
            pltpu.VMEM((CH, 256, 256), F32),
            pltpu.VMEM((256, POS), BF16),
            pltpu.VMEM((256, 256), F32),
        ],
        values.reshape(SEQS, BLOCKS, 16, 128),
        filt,
        skip,
    )
    back = lax.all_to_all(conv.reshape(256, 16, 128), both, split_axis=0, concat_axis=0, tiled=True)
    experts = jnp.arange(64, dtype=I32)
    rep = (spare_pick[(experts // 2 + 16) % 32] == experts % 2).astype(F32)
    send, hidden = call(
        norm_kernel,
        (sds((HOMES, MSG, QW), BF16), sds((TOK, WIDTH), F32)),
        [pltpu.VMEM((TOK, WIDTH), BF16), pltpu.VMEM((64, TOK), F32)],
        back.reshape(HOMES, GROUPS, 16, 128),
        resid,
        gate_in,
        rims,
        gate_short,
        norm_gain.reshape(1, WIDTH),
        expert_ids.T,
        rep.reshape(64, 1),
    )
    recv = lax.all_to_all(send, "expert", split_axis=0, concat_axis=0, tiled=True)
    hot = lax.dynamic_slice_in_dim(spare_pick, (me + 16) % 32, 1, 0)
    outs = call(ffn_kernel, sds((HOMES, MSG, QW), BF16), [], hot, recv, w_gate, w_up, w_down, smem=1)
    ret = lax.all_to_all(outs, "expert", split_axis=0, concat_axis=0, tiled=True)
    return call(
        combine_kernel,
        sds((TOK, WIDTH), BF16),
        [pltpu.VMEM((2, TOK, HOMES * MAIN), BF16), pltpu.VMEM((2, TOK, HOMES * 16), BF16)],
        ret,
        hidden,
        expert_ids,
        gate_wts,
        rep.reshape(1, 64),
    )


def solution(mesh):
    placed = (
        P(("expert", "seq"), None),
        P(("expert", "seq"), None),
        P(),
        P(),
        P("expert", "seq"),
        P("seq"),
        P(),
        P(("expert", "seq"), None),
        P(("expert", "seq"), None),
        P(),
        P("expert", None, None),
        P("expert", None, None),
        P("expert", None, None),
    )
    return jax.shard_map(
        body, mesh=mesh, in_specs=placed, out_specs=P(("expert", "seq"), None), check_vma=False
    )
```

```python
import functools

import jax
import jax.numpy as jnp
from jax import lax
from jax.experimental import pallas as pl
from jax.experimental.pallas import tpu as pltpu
from jax.sharding import PartitionSpec as P

F32, BF16, I32 = jnp.float32, jnp.bfloat16, jnp.int32
VMEM_LIMIT = 56 * 1024 * 1024
TOK = 256
WIDTH = 2048
HOMES = 32
GROUPS = 8
SEQS = 16
BLOCKS = 16
CH = 8
POS = SEQS * TOK
QUARTERS = 4
QW = WIDTH // QUARTERS
MAIN = 32
LEFT = 4
MSG = QUARTERS * (MAIN + LEFT)
CAP = 12
HID = 256
PAD = 128
NEAR = HOMES * GROUPS
PARTS = 4
PER = HOMES // PARTS
MESH = pl.DeviceIdType.MESH


def iota(shape, dim):
    return lax.broadcasted_iota(I32, shape, dim)


def eye(n):
    return (iota((n, n), 0) == iota((n, n), 1)).astype(BF16)


def nt(a, b):
    return lax.dot_general(a, b, (((1,), (1,)), ((), ())), preferred_element_type=F32)


def mm(a, b):
    return jnp.dot(a, b, preferred_element_type=F32)


def short_conv(x, before2, before1, kernel):
    row = iota(x.shape, 0)
    back1 = jnp.where(row == 0, before1, pltpu.roll(x, 1, 0))
    back2 = jnp.where(row == 0, before2, jnp.where(row == 1, before1, pltpu.roll(x, 2, 0)))
    return kernel[0:1] * x + kernel[1:2] * back1 + kernel[2:3] * back2


def group_cols(g):
    return pl.ds(pl.multiple_of(g * 256, 256), 256)


def to_message(block):
    first = block[:, :128].reshape(32, 8, 128)
    second = block[:, 128:].reshape(32, 8, 128)
    return jnp.concatenate([first, second], axis=1).astype(BF16)


def from_message(message):
    wide = message.astype(F32)
    first = wide[:, :8].reshape(256, 128).astype(BF16)
    second = wide[:, 8:].reshape(256, 128).astype(BF16)
    ident = eye(128)
    return jnp.concatenate([nt(ident, first), nt(ident, second)], axis=0)


def build_bank(row, bank_ref):
    wide = jnp.concatenate([jnp.broadcast_to(row, (8, POS)), jnp.zeros((8, PAD), F32)], axis=1)
    base = pltpu.roll(wide, 0, 1, stride=1, stride_axis=0)
    for a in range(8):
        upper = pltpu.roll(base, 16 * a, 1) if a else base
        lower = pltpu.roll(base, 16 * a + 8, 1)
        both = jnp.concatenate([upper, lower], axis=0)[:, :POS].astype(BF16)
        bank_ref[16 * a : 16 * a + 16, :] = both
        bank_ref[128 + 16 * a : 144 + 16 * a, PAD:] = both[:, : POS - PAD]


def slots(named, rep, axis):
    tri = (iota((TOK, TOK), axis) < iota((TOK, TOK), 1 - axis)).astype(BF16)
    if axis == 0:
        rank = mm(named.astype(BF16), tri)
    else:
        rank = mm(tri, named.astype(BF16))
    kept = (named > 0) & ((rank < CAP) | ((rank < 2 * CAP) & (rep > 0)))
    return jnp.where(kept, jnp.where(rep > 0, rank, rank + 2 * CAP), -1.0)


def silu_mul(gate, up):
    return gate / (1.0 + jnp.exp(-gate)) * up


def ffn_group(first, n, recv_ref, wg_ref, wu_ref, wd_ref, out_ref, hot):
    cold = 1 - hot
    src = pl.ds(first, n)
    rows = 16 * n
    zero = functools.partial(jnp.zeros, (rows, HID), F32)
    ga, ua, gb, ub, gc, uc, gl, ul = (zero() for _ in range(8))
    left = recv_ref[src, MAIN * QUARTERS :, :].reshape(rows, QW)
    part = iota((rows, HID), 0) % 16 // 4
    for q in range(QUARTERS):
        xa = recv_ref[src, MAIN * q : MAIN * q + 16, :].reshape(rows, QW)
        xb = recv_ref[src, MAIN * q + 16 : MAIN * q + 32, :].reshape(rows, QW)
        cut = slice(QW * q, QW * q + QW)
        both = jnp.concatenate([xa, xb], axis=0)
        gh, uh = mm(both, wg_ref[hot, cut, :]), mm(both, wu_ref[hot, cut, :])
        ga, ua, gb, ub = ga + gh[:rows], ua + uh[:rows], gb + gh[rows:], ub + uh[rows:]
        both = jnp.concatenate([xb, left], axis=0)
        gh, uh = mm(both, wg_ref[cold, cut, :]), mm(both, wu_ref[cold, cut, :])
        gc, uc = gc + gh[:rows], uc + uh[:rows]
        gl = gl + jnp.where(part == q, gh[rows:], 0.0)
        ul = ul + jnp.where(part == q, uh[rows:], 0.0)

    def over_quarters(acc):
        acc = acc.reshape(n, 16, HID)
        acc = acc[:, :8] + acc[:, 8:]
        acc = acc.reshape(8 * n, HID)
        low = iota(acc.shape, 0) % 8 < 4
        other = jnp.where(low, pltpu.roll(acc, 8 * n - 4, 0), pltpu.roll(acc, 4, 0))
        acc = (acc + other).reshape(n, 8, HID)
        return jnp.concatenate([acc, acc], axis=1).reshape(rows, HID)

    is_hot = iota((rows, HID), 0) % 16 < 8
    act_a = silu_mul(ga, ua).astype(BF16)
    act_b = silu_mul(jnp.where(is_hot, gb, gc), jnp.where(is_hot, ub, uc))
    act_bh = jnp.where(is_hot, act_b, 0.0).astype(BF16)
    act_bc = jnp.where(is_hot, 0.0, act_b).astype(BF16)
    act_l = silu_mul(over_quarters(gl), over_quarters(ul)).astype(BF16)
    hot_in = jnp.concatenate([act_a, act_bh], axis=0)
    cold_in = jnp.concatenate([act_bc, act_l], axis=0)
    part = iota((rows, QW), 0) % 16 // 4
    spill = jnp.zeros((rows, QW), F32)
    for q in range(QUARTERS):
        cut = slice(QW * q, QW * q + QW)
        oh = nt(hot_in, wd_ref[hot, cut, :])
        oc = nt(cold_in, wd_ref[cold, cut, :])
        out_ref[src, MAIN * q : MAIN * q + 16, :] = oh[:rows].astype(BF16).reshape(n, 16, QW)
        out_ref[src, MAIN * q + 16 : MAIN * q + 32, :] = (oh[rows:] + oc[:rows]).astype(BF16).reshape(n, 16, QW)
        spill = jnp.where(part == q, oc[rows:], spill)
    out_ref[src, MAIN * QUARTERS :, :] = spill.astype(BF16).reshape(n, 16, QW)


def partner(order):
    t = (order + 1) * 11 % 32
    return 2 * (t % 2) + t // 2 % 2, 2 * (t // 4 % 2) + t // 8 % 2, t // 16


def ahead(e, offset, sign):
    dx, dy, dc = offset
    x = (e // 8 + 4 + sign * dx) % 4
    y = (e // 2 % 4 + 4 + sign * dy) % 4
    return 8 * x + 2 * y + (e + dc) % 2


def far(step):
    t = step * 37 % NEAR
    q = t // GROUPS
    return (q // 8, q // 2 % 4, q % 2), t % GROUPS


def exchange_kernel(
    resid_ref, rim_ref, kern_ref, filt_ref, skip_ref, out_ref,
    vsend, vrecv, fsend, frecv, csend, crecv, wide_ref, hrow_ref, x_ref, bank_ref, acc_ref,
    f_ssem, f_rsem, v_ssem, v_rsem, c_ssem, c_rsem,
):
    e, z = lax.axis_index("expert"), lax.axis_index("seq")
    barrier = pltpu.get_barrier_semaphore()

    def greet(step, _):
        offset, dz = far(step)
        target = (ahead(e, offset, 1), (z + dz) % GROUPS)
        pl.semaphore_signal(barrier, inc=1, device_id=target, device_id_type=MESH)
        return 0

    lax.fori_loop(1, NEAR, greet, 0)
    ident = eye(256)
    fsend[...] = nt(ident, filt_ref[...]).reshape(HOMES, CH, 128)

    def one(g, _):
        cols = group_cols(g)
        x = resid_ref[:, cols].astype(F32)
        values = short_conv(x, rim_ref[2:3, cols], rim_ref[3:4, cols], kern_ref[:, cols]).astype(BF16)
        vsend[g] = to_message(nt(ident, values))
        return 0

    lax.fori_loop(0, GROUPS, one, 0)
    pl.semaphore_wait(barrier, NEAR - 1)

    def send_filter(order, _):
        target = ahead(e, partner(order), 1)
        pltpu.make_async_remote_copy(
            src_ref=fsend.at[target], dst_ref=frecv.at[e], send_sem=f_ssem, recv_sem=f_rsem,
            device_id=(target, z), device_id_type=MESH,
        ).start()
        return 0

    lax.fori_loop(0, HOMES - 1, send_filter, 0)
    row = (e % 2 * GROUPS + z) * SEQS + e // 2

    def send_values(step, _):
        offset, dz = far(step)
        target, there = ahead(e, offset, 1), (z + dz) % GROUPS
        pltpu.make_async_remote_copy(
            src_ref=vsend.at[there, target], dst_ref=vrecv.at[row], send_sem=v_ssem, recv_sem=v_rsem,
            device_id=(target, there), device_id_type=MESH,
        ).start()
        return 0

    lax.fori_loop(1, NEAR, send_values, 0)
    frecv[e] = fsend[e]
    vrecv[row] = vsend[z, e]
    some = frecv.at[pl.ds(0, HOMES - 1)]
    pltpu.make_async_copy(some, some, f_rsem).wait()
    for d in range(HOMES):
        hrow_ref[:, 128 * d : 128 * d + 128] = frecv[d]
    bank_ref[:, 128:, :PAD] = jnp.zeros((CH, 128, PAD), BF16)

    def bank(c, _):
        build_bank(hrow_ref[pl.ds(c, 1), :], bank_ref.at[c])
        return 0

    lax.fori_loop(0, CH, bank, 0)
    some = vrecv.at[pl.ds(0, NEAR - 1)]
    pltpu.make_async_copy(some, some, v_rsem).wait()

    def widen(i, _):
        wide_ref[pl.ds(pl.multiple_of(i * 256, 256), 256)] = vrecv[pl.ds(i * 16, 16)].astype(F32).reshape(256, 128)
        return 0

    lax.fori_loop(0, BLOCKS, widen, 0)
    for c in range(CH):
        for half in range(2):
            x_ref[c, :, 128 * half : 128 * half + 128] = wide_ref[pl.ds(8 * half + c, 256, stride=16), :]

    def conv(c, _):
        x = x_ref[c]
        lhs = x.astype(BF16)
        acc_ref[...] = x * skip_ref[pl.ds(c, 1), :]
        for k in range(BLOCKS):
            acc_ref[16 * k :, :] += mm(lhs[: 256 - 16 * k], bank_ref[c, :, 256 * k : 256 * k + 256])
        x_ref[c] = acc_ref[...]
        return 0

    lax.fori_loop(0, CH, conv, 0)
    for c in range(CH):
        for half in range(2):
            wide_ref[pl.ds(8 * half + c, 256, stride=16), :] = x_ref[c, :, 128 * half : 128 * half + 128]

    def narrow(i, _):
        csend[pl.ds(i * 16, 16)] = wide_ref[pl.ds(pl.multiple_of(i * 256, 256), 256)].reshape(16, 16, 128).astype(BF16)
        return 0

    lax.fori_loop(0, BLOCKS, narrow, 0)

    def send_back(step, _):
        offset, dz = far(step)
        target, there = ahead(e, offset, 1), (z + dz) % GROUPS
        place = (target % 2 * GROUPS + there) * SEQS + target // 2
        pltpu.make_async_remote_copy(
            src_ref=csend.at[place], dst_ref=crecv.at[z, e], send_sem=c_ssem, recv_sem=c_rsem,
            device_id=(target, there), device_id_type=MESH,
        ).start()
        return 0

    lax.fori_loop(1, NEAR, send_back, 0)
    crecv[z, e] = csend[row]
    some = fsend.at[pl.ds(0, HOMES - 1)]
    pltpu.make_async_copy(some, some, f_ssem).wait()
    some = csend.at[pl.ds(0, NEAR - 1)]
    pltpu.make_async_copy(some, some, v_ssem).wait()
    pltpu.make_async_copy(some, some, c_rsem).wait()
    pltpu.make_async_copy(some, some, c_ssem).wait()
    out_ref[...] = crecv[...]


def prepare_weights(ids_ref, wts_ref, rep_ref, slot_ref, weight_ref):
    named = jnp.zeros((TOK, 64), F32)
    weight = jnp.zeros((TOK, 64), F32)
    for k in range(4):
        hit = ids_ref[:, k : k + 1] == iota((TOK, 64), 1)
        named += hit.astype(F32)
        weight += jnp.where(hit, wts_ref[:, k : k + 1], 0.0)
    slot_ref[...] = slots(named, rep_ref[...], 1).astype(BF16)
    high = weight.astype(BF16)
    weight_ref[0] = high
    weight_ref[1] = (weight - high.astype(F32)).astype(BF16)


def part_weights(e, g, per, want, slot_ref, weight_ref):
    shape = (64, PER * per)
    home = ahead(e, partner(PER * g + iota(shape, 1) // per), 1)
    high = low = jnp.zeros((TOK, PER * per), F32)
    for odd in range(2):
        pick = (iota(shape, 0) == 2 * home + odd).astype(BF16)
        hit = mm(slot_ref[...], pick) == want
        high = high + jnp.where(hit, mm(weight_ref[0], pick), 0.0)
        low = low + jnp.where(hit, mm(weight_ref[1], pick), 0.0)
    return high.astype(BF16), low.astype(BF16)


def experts_kernel(
    hot_ref, back_ref, resid_ref, gate_in_ref, rim_ref, kern_ref, gain_ref, idst_ref, ids_ref, wts_ref, repc_ref, repr_ref,
    wg_ref, wu_ref, wd_ref, out_ref,
    hid_ref, normed_ref, slott_ref, slot_ref, weight_ref, wmain_ref, wleft_ref, send, recv, give, ret,
    d_ssem, d_rsem, r_ssem, r_rsem,
):
    e, z = lax.axis_index("expert"), lax.axis_index("seq")
    barrier = pltpu.get_barrier_semaphore()

    def greet(order, _):
        target = (ahead(e, partner(order), 1), z)
        pl.semaphore_signal(barrier, inc=1, device_id=target, device_id_type=MESH)
        return 0

    lax.fori_loop(0, HOMES - 1, greet, 0)

    def one(g, total):
        cols = group_cols(g)
        x = gate_in_ref[:, cols].astype(F32)
        gated = short_conv(x, rim_ref[0:1, cols], rim_ref[1:2, cols], kern_ref[:, cols])
        hidden = resid_ref[:, cols].astype(F32) + gated * from_message(back_ref[g])
        hid_ref[:, cols] = hidden
        return total + jnp.sum(hidden * hidden, axis=1, keepdims=True)

    total = lax.fori_loop(0, GROUPS, one, jnp.zeros((TOK, 1), F32))
    scale = lax.rsqrt(total * (1.0 / WIDTH) + 1e-05)

    def two(g, _):
        cols = group_cols(g)
        normed_ref[:, cols] = (hid_ref[:, cols] * scale * gain_ref[:, cols]).astype(BF16)
        return 0

    lax.fori_loop(0, GROUPS, two, 0)
    named = jnp.zeros((64, TOK), F32)
    for k in range(4):
        named += (idst_ref[k : k + 1, :] == iota((64, TOK), 0)).astype(F32)
    slott_ref[...] = slots(named, repc_ref[...], 0)
    pl.semaphore_wait(barrier, HOMES - 1)

    def move(source, sink, order, sign, ssem, rsem):
        pltpu.make_async_remote_copy(
            src_ref=source.at[order], dst_ref=sink.at[order], send_sem=ssem, recv_sem=rsem,
            device_id=(ahead(e, partner(order), sign), z), device_id_type=MESH,
        ).start()

    def move_part(source, sink, g, sign, ssem, rsem):
        for j in range(PER - 1):
            move(source, sink, PER * g + j, sign, ssem, rsem.at[g])

        @pl.when(g < PARTS - 1)
        def _():
            move(source, sink, PER * g + PER - 1, sign, ssem, rsem.at[g])

        @pl.when(g == PARTS - 1)
        def _():
            pltpu.make_async_copy(source.at[HOMES - 1], sink.at[HOMES - 1], rsem.at[g]).start()

    def wait_part(sink, g, rsem):
        part = sink.at[pl.ds(PER * g, PER)]
        pltpu.make_async_copy(part, part, rsem.at[g]).wait()

    def dispatch(g, _):
        sel = []
        left = []
        for j in range(PER):
            home = ahead(e, partner(PER * g + j), 1)
            even = slott_ref[pl.ds(2 * home, 1), :]
            odd = slott_ref[pl.ds(2 * home + 1, 1), :]
            r = iota((MAIN, TOK), 0).astype(F32)
            sel.append(((even == r) | (odd == r)).astype(BF16))
            r = (iota((16, TOK), 0) % 4 + MAIN).astype(F32)
            left.append(((even == r) | (odd == r)).astype(F32))
        sel = jnp.concatenate(sel, axis=0)
        left = jnp.concatenate(left, axis=0)
        part = iota((16 * PER, TOK), 0) % 16 // 4
        spill = jnp.zeros((16 * PER, QW), F32)
        for q in range(QUARTERS):
            cols = normed_ref[:, QW * q : QW * q + QW]
            send[pl.ds(PER * g, PER), MAIN * q : MAIN * q + MAIN, :] = mm(sel, cols).astype(BF16).reshape(PER, MAIN, QW)
            spill += mm(jnp.where(part == q, left, 0.0).astype(BF16), cols)
        send[pl.ds(PER * g, PER), MAIN * QUARTERS :, :] = spill.astype(BF16).reshape(PER, 16, QW)
        move_part(send, recv, g, 1, d_ssem, d_rsem)
        return 0

    lax.fori_loop(0, PARTS, dispatch, 0)
    prepare_weights(ids_ref, wts_ref, repr_ref, slot_ref, weight_ref)

    def weigh(g, _):
        want = (iota((TOK, PER * MAIN), 1) % MAIN).astype(F32)
        wmain_ref[g, 0], wmain_ref[g, 1] = part_weights(e, g, MAIN, want, slot_ref, weight_ref)
        want = (iota((TOK, PER * 16), 1) % 4 + MAIN).astype(F32)
        wleft_ref[g, 0], wleft_ref[g, 1] = part_weights(e, g, 16, want, slot_ref, weight_ref)
        return 0

    lax.fori_loop(0, PARTS, weigh, 0)
    hot = hot_ref[0]

    def expert(g, _):
        wait_part(recv, g, d_rsem)
        ffn_group(PER * g, PER, recv, wg_ref, wu_ref, wd_ref, give, hot)
        move_part(give, ret, g, -1, r_ssem, r_rsem)
        return 0

    lax.fori_loop(0, PARTS, expert, 0)

    def combine(g, _):
        wait_part(ret, g, r_rsem)
        left = ret[pl.ds(PER * g, PER), MAIN * QUARTERS :, :].reshape(PER * 16, QW)
        part = iota((TOK, PER * 16), 1) % 16 // 4
        for q in range(QUARTERS):
            main = ret[pl.ds(PER * g, PER), MAIN * q : MAIN * q + MAIN, :].reshape(PER * MAIN, QW)
            moe = mm(wmain_ref[g, 0], main) + mm(wmain_ref[g, 1], main)
            for w in range(2):
                moe += mm(jnp.where(part == q, wleft_ref[g, w].astype(F32), 0.0).astype(BF16), left)
            cut = slice(QW * q, QW * q + QW)
            hid_ref[:, cut] += moe
        return 0

    lax.fori_loop(0, PARTS, combine, 0)
    some = send.at[pl.ds(0, HOMES - 1)]
    pltpu.make_async_copy(some, some, d_ssem).wait()
    pltpu.make_async_copy(some, some, r_ssem).wait()
    out_ref[...] = hid_ref[...].astype(BF16)


def whole(n):
    return [pl.BlockSpec(memory_space=pltpu.VMEM)] * n


def call(kernel, outs, scratch, *args, cid, smem=0):
    return pl.pallas_call(
        kernel,
        out_shape=outs,
        in_specs=[pl.BlockSpec(memory_space=pltpu.SMEM)] * smem + whole(len(args) - smem),
        out_specs=whole(1)[0] if not isinstance(outs, tuple) else tuple(whole(len(outs))),
        scratch_shapes=scratch,
        compiler_params=pltpu.CompilerParams(
            vmem_limit_bytes=VMEM_LIMIT, collective_id=cid, has_side_effects=True
        ),
    )(*args)


def body(
    resid,
    gate_in,
    gate_short,
    value_short,
    long_filter,
    skip_gain,
    norm_gain,
    expert_ids,
    gate_wts,
    spare_pick,
    w_gate,
    w_up,
    w_down,
):
    n_seq = lax.axis_size("seq")
    n_exp = lax.axis_size("expert")
    me = lax.axis_index("expert")
    z = lax.axis_index("seq")
    tails = jnp.stack([gate_in[-2:], resid[-2:]])
    count = n_exp * n_seq
    rims = lax.ppermute(tails, ("expert", "seq"), [(i, i + 1) for i in range(count - 1)])
    rims = jnp.where((z == 0) & (me % 2 == 0), jnp.zeros((), BF16), rims)
    rims = rims.astype(F32).reshape(4, WIDTH)
    sds = jax.ShapeDtypeStruct
    skip = lax.dynamic_slice_in_dim(skip_gain, me * CH, CH, 0)
    skip = jnp.broadcast_to(skip[:, None], (CH, 256))
    experts = jnp.arange(64, dtype=I32)
    rep = (spare_pick[(experts // 2 + 16) % 32] == experts % 2).astype(F32)
    hot = lax.dynamic_slice_in_dim(spare_pick, (me + 16) % 32, 1, 0)
    dma = pltpu.SemaphoreType.DMA
    back = call(
        exchange_kernel,
        sds((GROUPS, HOMES, 16, 128), BF16),
        [
            pltpu.VMEM((GROUPS, HOMES, 16, 128), BF16),
            pltpu.VMEM((NEAR, 16, 128), BF16),
            pltpu.VMEM((HOMES, CH, 128), F32),
            pltpu.VMEM((HOMES, CH, 128), F32),
            pltpu.VMEM((NEAR, 16, 128), BF16),
            pltpu.VMEM((GROUPS, HOMES, 16, 128), BF16),
            pltpu.VMEM((POS, 128), F32),
            pltpu.VMEM((CH, POS), F32),
            pltpu.VMEM((CH, 256, 256), F32),
            pltpu.VMEM((CH, 256, POS), BF16),
            pltpu.VMEM((256, 256), F32),
        ]
        + [dma] * 6,
        resid,
        rims,
        value_short,
        long_filter,
        skip,
        cid=0,
    )
    message = pltpu.VMEM((HOMES, MSG, QW), BF16)
    return call(
        experts_kernel,
        sds((TOK, WIDTH), BF16),
        [
            pltpu.VMEM((TOK, WIDTH), F32),
            pltpu.VMEM((TOK, WIDTH), BF16),
            pltpu.VMEM((64, TOK), F32),
            pltpu.VMEM((TOK, 64), BF16),
            pltpu.VMEM((2, TOK, 64), BF16),
            pltpu.VMEM((PARTS, 2, TOK, PER * MAIN), BF16),
            pltpu.VMEM((PARTS, 2, TOK, PER * 16), BF16),
            message,
            message,
            message,
            message,
            dma,
            dma((PARTS,)),
            dma,
            dma((PARTS,)),
        ],
        hot,
        back,
        resid,
        gate_in,
        rims,
        gate_short,
        norm_gain.reshape(1, WIDTH),
        expert_ids.T,
        expert_ids,
        gate_wts,
        rep.reshape(64, 1),
        rep.reshape(1, 64),
        w_gate,
        w_up,
        w_down,
        smem=1,
        cid=1,
    )


def solution(mesh):
    placed = (
        P(("expert", "seq"), None),
        P(("expert", "seq"), None),
        P(),
        P(),
        P("expert", "seq"),
        P("seq"),
        P(),
        P(("expert", "seq"), None),
        P(("expert", "seq"), None),
        P(),
        P("expert", None, None),
        P("expert", None, None),
        P("expert", None, None),
    )
    return jax.shard_map(
        body, mesh=mesh, in_specs=placed, out_specs=P(("expert", "seq"), None), check_vma=False
    )
```

```python
import functools

import jax
import jax.numpy as jnp
from jax import lax
from jax.experimental import pallas as pl
from jax.experimental.pallas import tpu as pltpu
from jax.sharding import PartitionSpec as P

F32, BF16, I32 = jnp.float32, jnp.bfloat16, jnp.int32
VMEM_LIMIT = 60 * 1024 * 1024
TOK = 256
WIDTH = 2048
HOMES = 32
GROUPS = 8
SEQS = 16
BLOCKS = 16
CH = 8
POS = SEQS * TOK
QUARTERS = 4
QW = WIDTH // QUARTERS
MAIN = 32
LEFT = 4
MSG = QUARTERS * (MAIN + LEFT)
CAP = 12
HID = 256
PAD = 128
NEAR = HOMES * GROUPS
PARTS = 4
PER = HOMES // PARTS
MESH = pl.DeviceIdType.MESH


def iota(shape, dim):
    return lax.broadcasted_iota(I32, shape, dim)


def eye(n):
    return (iota((n, n), 0) == iota((n, n), 1)).astype(BF16)


def nt(a, b):
    return lax.dot_general(a, b, (((1,), (1,)), ((), ())), preferred_element_type=F32)


def mm(a, b):
    return jnp.dot(a, b, preferred_element_type=F32)


def short_conv(x, before2, before1, kernel):
    row = iota(x.shape, 0)
    back1 = jnp.where(row == 0, before1, pltpu.roll(x, 1, 0))
    back2 = jnp.where(row == 0, before2, jnp.where(row == 1, before1, pltpu.roll(x, 2, 0)))
    return kernel[0:1] * x + kernel[1:2] * back1 + kernel[2:3] * back2


def group_cols(g):
    return pl.ds(pl.multiple_of(g * 256, 256), 256)


def to_message(block):
    first = block[:, :128].reshape(32, 8, 128)
    second = block[:, 128:].reshape(32, 8, 128)
    return jnp.concatenate([first, second], axis=1).astype(BF16)


def from_message(message):
    wide = message.astype(F32)
    first = wide[:, :8].reshape(256, 128).astype(BF16)
    second = wide[:, 8:].reshape(256, 128).astype(BF16)
    ident = eye(128)
    return jnp.concatenate([nt(ident, first), nt(ident, second)], axis=0)


def partner(order):
    t = (order + 1) * 11 % 32
    return 2 * (t % 2) + t // 2 % 2, 2 * (t // 4 % 2) + t // 8 % 2, t // 16


def ahead(e, offset, sign):
    dx, dy, dc = offset
    x = (e // 8 + 4 + sign * dx) % 4
    y = (e // 2 % 4 + 4 + sign * dy) % 4
    return 8 * x + 2 * y + (e + dc) % 2


def slots(named, rep, axis):
    tri = (iota((TOK, TOK), axis) < iota((TOK, TOK), 1 - axis)).astype(BF16)
    if axis == 0:
        rank = mm(named.astype(BF16), tri)
    else:
        rank = mm(tri, named.astype(BF16))
    kept = (named > 0) & ((rank < CAP) | ((rank < 2 * CAP) & (rep > 0)))
    return jnp.where(kept, jnp.where(rep > 0, rank, rank + 2 * CAP), -1.0)


def prepare_routing(spare_ref, idst_ref, wtst_ref, slott_ref, slot_ref, weight_ref):
    expert, index = iota((64, HOMES), 0), iota((64, HOMES), 1)
    picked = jnp.where(index == (expert // 2 + 16) % 32, spare_ref[...], 0)
    rep = jnp.sum(picked.astype(F32), axis=1, keepdims=True) == (iota((64, 1), 0) % 2).astype(F32)
    named = jnp.zeros((64, TOK), F32)
    weight = jnp.zeros((64, TOK), F32)
    for k in range(4):
        hit = idst_ref[k : k + 1, :] == iota((64, TOK), 0)
        named += hit.astype(F32)
        weight += jnp.where(hit, wtst_ref[k : k + 1, :], 0.0)
    slot = slots(named, rep.astype(F32), 0)
    slott_ref[...] = slot
    ident = eye(TOK)
    slot_ref[...] = nt(ident, slot.astype(BF16)).astype(BF16)
    high = weight.astype(BF16)
    weight_ref[0] = nt(ident, high).astype(BF16)
    weight_ref[1] = nt(ident, (weight - high.astype(F32)).astype(BF16)).astype(BF16)


def part_picks(e, g, per):
    shape = (64, PER * per)
    home = ahead(e, partner(PER * g + iota(shape, 1) // per), 1)
    return [(iota(shape, 0) == 2 * home + odd).astype(BF16) for odd in range(2)]


def part_hits(e, g, per, want, slot_ref):
    return [mm(slot_ref[...], pick) == want for pick in part_picks(e, g, per)]


def part_weights(e, g, per, want, slot_ref, weight_ref):
    high = low = jnp.zeros((TOK, PER * per), F32)
    for pick in part_picks(e, g, per):
        hit = mm(slot_ref[...], pick) == want
        high = high + jnp.where(hit, mm(weight_ref[0], pick), 0.0)
        low = low + jnp.where(hit, mm(weight_ref[1], pick), 0.0)
    return high.astype(BF16), low.astype(BF16)


def build_bank(row, bank_ref):
    wide = jnp.concatenate([jnp.broadcast_to(row, (8, POS)), jnp.zeros((8, PAD), F32)], axis=1)
    base = pltpu.roll(wide, 0, 1, stride=1, stride_axis=0)
    for a in range(8):
        upper = pltpu.roll(base, 16 * a, 1) if a else base
        lower = pltpu.roll(base, 16 * a + 8, 1)
        both = jnp.concatenate([upper, lower], axis=0)[:, :POS].astype(BF16)
        bank_ref[16 * a : 16 * a + 16, PAD:] = both


def arrival(i):
    return jnp.where(i % 2 == 1, (i + 1) // 2, GROUPS - i // 2) % GROUPS


def silu_mul(gate, up):
    return gate / (1.0 + jnp.exp(-gate)) * up


def scale_columns(g, scales, lanes_of, per):
    cols = []
    for j in range(PER):
        sub, lane, rows = lanes_of(j)
        line = scales[PER * g + j, sub : sub + 1, :]
        hit = iota((per, 128), 1) == lane + iota((per, 128), 0)
        cols.append(jnp.sum(jnp.where(hit, line, 0.0), axis=1, keepdims=True))
    return jnp.concatenate(cols, axis=0)


def ffn_group(g, groups, scales, recv_ref, wg_ref, wu_ref, wd_ref, out_ref, hot):
    cold = 1 - hot
    n = PER
    src = pl.ds(g * PER, n)
    rows = 16 * n
    zero = functools.partial(jnp.zeros, (rows, HID), F32)
    ga, ua, gb, ub, gc, uc, gl, ul = (zero() for _ in range(8))
    part = iota((rows, HID), 0) % 16 // 4
    for i in range(GROUPS):
        q = i // 2
        lanes = slice(256 * (i % 2), 256 * (i % 2) + 256)
        xa = recv_ref[src, MAIN * q : MAIN * q + 16, lanes].reshape(rows, 256)
        xb = recv_ref[src, MAIN * q + 16 : MAIN * q + 32, lanes].reshape(rows, 256)
        left = recv_ref[src, MAIN * QUARTERS :, lanes].reshape(rows, 256)
        cut = group_cols(groups[i])
        both = jnp.concatenate([xa, xb], axis=0)
        gh, uh = mm(both, wg_ref[hot, cut, :]), mm(both, wu_ref[hot, cut, :])
        ga, ua, gb, ub = ga + gh[:rows], ua + uh[:rows], gb + gh[rows:], ub + uh[rows:]
        both = jnp.concatenate([xb, left], axis=0)
        gh, uh = mm(both, wg_ref[cold, cut, :]), mm(both, wu_ref[cold, cut, :])
        gc, uc = gc + gh[:rows], uc + uh[:rows]
        gl = gl + jnp.where(part == q, gh[rows:], 0.0)
        ul = ul + jnp.where(part == q, uh[rows:], 0.0)

    def over_quarters(acc):
        acc = acc.reshape(n, 16, HID)
        acc = acc[:, :8] + acc[:, 8:]
        acc = acc.reshape(8 * n, HID)
        low = iota(acc.shape, 0) % 8 < 4
        other = jnp.where(low, pltpu.roll(acc, 8 * n - 4, 0), pltpu.roll(acc, 4, 0))
        acc = (acc + other).reshape(n, 8, HID)
        return jnp.concatenate([acc, acc], axis=1).reshape(rows, HID)

    sa = scale_columns(g, scales, lambda j: (j // 4, 32 * (j % 4), 16), 16)
    sb = scale_columns(g, scales, lambda j: (j // 4, 32 * (j % 4) + 16, 16), 16)
    sl = scale_columns(g, scales, lambda j: (2, 16 * j, 16), 16)
    is_hot = iota((rows, HID), 0) % 16 < 8
    act_a = silu_mul(ga * sa, ua * sa).astype(BF16)
    act_b = silu_mul(jnp.where(is_hot, gb, gc) * sb, jnp.where(is_hot, ub, uc) * sb)
    act_bh = jnp.where(is_hot, act_b, 0.0).astype(BF16)
    act_bc = jnp.where(is_hot, 0.0, act_b).astype(BF16)
    act_l = silu_mul(over_quarters(gl) * sl, over_quarters(ul) * sl).astype(BF16)
    hot_in = jnp.concatenate([act_a, act_bh], axis=0)
    cold_in = jnp.concatenate([act_bc, act_l], axis=0)
    part = iota((rows, 256), 0) % 16 // 4
    spill = [jnp.zeros((rows, 256), F32)] * 2
    for i in range(GROUPS):
        q = i // 2
        lanes = slice(256 * (i % 2), 256 * (i % 2) + 256)
        cut = group_cols(groups[i])
        oh = nt(hot_in, wd_ref[hot, cut, :])
        oc = nt(cold_in, wd_ref[cold, cut, :])
        out_ref[src, MAIN * q : MAIN * q + 16, lanes] = oh[:rows].astype(BF16).reshape(n, 16, 256)
        out_ref[src, MAIN * q + 16 : MAIN * q + 32, lanes] = (oh[rows:] + oc[:rows]).astype(BF16).reshape(n, 16, 256)
        spill[i % 2] = jnp.where(part == q, oc[rows:], spill[i % 2])
    out_ref[src, MAIN * QUARTERS :, :] = jnp.concatenate(spill, axis=1).astype(BF16).reshape(n, 16, QW)


def layer_kernel(
    spare_ref, skip_ref, resid_ref, gate_in_ref, gate_kern_ref, value_kern_ref, filt_ref, gain_ref, idst_ref, wtst_ref,
    row_ref, wg_hbm, wu_hbm, wd_hbm, out_ref,
    vsend, vrecv, fsend, frecv, csend, crecv, rims, wide_ref, hrow_ref, x_ref, bank_ref, acc_ref,
    hid_ref, normed_ref, slott_ref, slot_ref, weight_ref, sel_ref, left_ref, wmain_ref, wleft_ref,
    send, recv, give, ret, ssend, srecv, wg_ref, wu_ref, wd_ref,
    b_sem, w_sem, t_ssem, t_rsem, f_ssem, f_rsem, v_ssem, v_rsem, c_ssem, c_rsem, s_ssem, s_rsem, d_ssem, d_rsem, r_ssem, r_rsem,
):
    e, z = lax.axis_index("expert"), lax.axis_index("seq")

    def device(order, sign=1):
        return ahead(e, partner(order), sign)

    def remote(source, sink, ssem, rsem, expert, seq):
        pltpu.make_async_remote_copy(
            src_ref=source, dst_ref=sink, send_sem=ssem, recv_sem=rsem, device_id=(expert, seq), device_id_type=MESH
        ).start()

    def await_bytes(ref, sem):
        pltpu.make_async_copy(ref, ref, sem).wait()

    barrier = pltpu.get_barrier_semaphore()

    def greet_line(dz, _):
        pl.semaphore_signal(barrier, inc=1, device_id=(e, (z + dz) % GROUPS), device_id_type=MESH)
        return 0

    def greet_plane(order, _):
        pl.semaphore_signal(barrier, inc=1, device_id=(device(order), z), device_id_type=MESH)
        return 0

    lax.fori_loop(1, GROUPS, greet_line, 0)
    lax.fori_loop(0, HOMES - 1, greet_plane, 0)
    weights = [
        pltpu.make_async_copy(hbm, vmem, w_sem.at[i])
        for i, (hbm, vmem) in enumerate(((wg_hbm, wg_ref), (wu_hbm, wu_ref), (wd_hbm, wd_ref)))
    ]
    for copy in weights:
        copy.start()
    ident = eye(256)
    fsend[...] = nt(ident, filt_ref[...]).reshape(HOMES, CH, 128)
    pl.semaphore_wait(barrier, GROUPS - 1 + HOMES - 1)

    def greet_again(dz, _):
        pl.semaphore_signal(b_sem, inc=1, device_id=(e, (z + dz) % GROUPS), device_id_type=MESH)
        return 0

    lax.fori_loop(1, GROUPS, greet_again, 0)
    pl.semaphore_wait(b_sem, GROUPS - 1)

    following = ((e + (z + 1) // GROUPS) % HOMES, (z + 1) % GROUPS)
    remote(gate_in_ref.at[pl.ds(TOK - 16, 16)], rims.at[0], t_ssem.at[0], t_rsem.at[0], *following)
    remote(resid_ref.at[pl.ds(TOK - 16, 16)], rims.at[1], t_ssem.at[1], t_rsem.at[1], *following)

    def send_filter(order, _):
        target = device(order)
        remote(fsend.at[target], frecv.at[e], f_ssem, f_rsem, target, z)
        return 0

    lax.fori_loop(0, HOMES - 1, send_filter, 0)
    frecv[e] = fsend[e]
    at_start = (z == 0) & (e % 2 == 0)

    def branch(ref, which, cols, kernel):
        tail = rims[which, :, cols].astype(F32)
        tail = jnp.where(at_start, 0.0, tail)
        return short_conv(ref[:, cols].astype(F32), tail[14:15], tail[15:16], kernel)

    await_bytes(rims.at[0], t_rsem.at[0])
    await_bytes(rims.at[1], t_rsem.at[1])
    row = (e % 2 * GROUPS + z) * SEQS + e // 2

    def make_values(r, _):
        there = (z + 3 * r + 4) % GROUPS
        cols = group_cols(there)
        values = branch(resid_ref, 1, cols, value_kern_ref[:, cols]).astype(BF16)
        vsend[there] = to_message(nt(ident, values))

        def send_values(order, _):
            target = device(order)
            remote(vsend.at[there, target], vrecv.at[row], v_ssem, v_rsem, target, there)
            return 0

        lax.fori_loop(0, HOMES - 1, send_values, 0)

        @pl.when(there != z)
        def _():
            remote(vsend.at[there, e], vrecv.at[row], v_ssem, v_rsem, e, there)

        return 0

    lax.fori_loop(0, GROUPS, make_values, 0)
    vrecv[row] = vsend[z, e]

    await_bytes(frecv.at[pl.ds(0, HOMES - 1)], f_rsem)
    for d in range(HOMES):
        hrow_ref[:, 128 * d : 128 * d + 128] = frecv[d]
    bank_ref[:, :, :PAD] = jnp.zeros((CH, 128, PAD), BF16)

    def bank(c, _):
        build_bank(hrow_ref[pl.ds(c, 1), :], bank_ref.at[c])
        return 0

    lax.fori_loop(0, CH, bank, 0)
    prepare_routing(row_ref, idst_ref, wtst_ref, slott_ref, slot_ref, weight_ref)

    def select(g, _):
        sel = []
        left = []
        for j in range(PER):
            home = device(PER * g + j)
            even = slott_ref[pl.ds(2 * home, 1), :]
            odd = slott_ref[pl.ds(2 * home + 1, 1), :]
            r = iota((MAIN, TOK), 0).astype(F32)
            sel.append(((even == r) | (odd == r)).astype(BF16))
            r = (iota((16, TOK), 0) % 4 + MAIN).astype(F32)
            left.append(((even == r) | (odd == r)).astype(BF16))
        sel_ref[g] = jnp.concatenate(sel, axis=0)
        left_ref[g] = jnp.concatenate(left, axis=0)
        want = (iota((TOK, PER * MAIN), 1) % MAIN).astype(F32)
        wmain_ref[g, 0], wmain_ref[g, 1] = part_weights(e, g, MAIN, want, slot_ref, weight_ref)
        want = (iota((TOK, PER * 16), 1) % 4 + MAIN).astype(F32)
        wleft_ref[g, 0], wleft_ref[g, 1] = part_weights(e, g, 16, want, slot_ref, weight_ref)
        return 0

    lax.fori_loop(0, PARTS, select, 0)
    await_bytes(vrecv.at[pl.ds(0, NEAR - 1)], v_rsem)

    def widen(i, _):
        wide_ref[pl.ds(pl.multiple_of(i * 256, 256), 256)] = vrecv[pl.ds(i * 16, 16)].astype(F32).reshape(256, 128)
        return 0

    lax.fori_loop(0, BLOCKS, widen, 0)
    for c in range(CH):
        for half in range(2):
            x_ref[c, :, 128 * half : 128 * half + 128] = wide_ref[pl.ds(8 * half + c, 256, stride=16), :]

    def conv(c, _):
        x = x_ref[c]
        lhs = x.astype(BF16)
        acc_ref[...] = x * skip_ref[e * CH + c]
        for k in range(BLOCKS):
            upper = bank_ref[c, :, PAD + 256 * k : PAD + 256 * k + 256]
            lower = bank_ref[c, :, 256 * k : 256 * k + 256]
            acc_ref[16 * k :, :] += mm(lhs[: 256 - 16 * k], jnp.concatenate([upper, lower], axis=0))
        x_ref[c] = acc_ref[...]
        return 0

    lax.fori_loop(0, CH, conv, 0)
    for c in range(CH):
        for half in range(2):
            wide_ref[pl.ds(8 * half + c, 256, stride=16), :] = x_ref[c, :, 128 * half : 128 * half + 128]

    def narrow(i, _):
        csend[pl.ds(i * 16, 16)] = wide_ref[pl.ds(pl.multiple_of(i * 256, 256), 256)].reshape(16, 16, 128).astype(BF16)
        return 0

    lax.fori_loop(0, BLOCKS, narrow, 0)

    def send_back(i, _):
        there = (z + arrival(i)) % GROUPS

        def send_plane(order, _):
            target = device(order)
            place = (target % 2 * GROUPS + there) * SEQS + target // 2
            remote(csend.at[place], crecv.at[i, e], c_ssem, c_rsem.at[i], target, there)
            return 0

        lax.fori_loop(0, HOMES - 1, send_plane, 0)

        @pl.when(there != z)
        def _():
            place = (e % 2 * GROUPS + there) * SEQS + e // 2
            remote(csend.at[place], crecv.at[i, e], c_ssem, c_rsem.at[i], e, there)

        return 0

    lax.fori_loop(0, GROUPS, send_back, 0)
    pltpu.make_async_copy(csend.at[row], crecv.at[0, e], c_rsem.at[0]).start()

    groups = [(z + GROUPS - arrival(jnp.int32(i))) % GROUPS for i in range(GROUPS)]

    def take(i, total):
        group = (z + GROUPS - arrival(i)) % GROUPS
        cols, mine = group_cols(group), group_cols(i)
        gated = branch(gate_in_ref, 0, cols, gate_kern_ref[:, cols])
        hidden = resid_ref[:, cols].astype(F32) + gated * from_message(crecv[i])
        hid_ref[:, mine] = hidden
        normed_ref[:, mine] = (hidden * gain_ref[:, cols]).astype(BF16)
        return total + jnp.sum(hidden * hidden, axis=1, keepdims=True)

    def take_two(q, total):
        await_bytes(crecv.at[2 * q], c_rsem.at[2 * q])
        total = take(2 * q, total)
        await_bytes(crecv.at[2 * q + 1], c_rsem.at[2 * q + 1])
        return take(2 * q + 1, total)

    def main_rows(q, g):
        cols = pl.ds(pl.multiple_of(QW * q, QW), QW)
        block = mm(sel_ref[g], normed_ref[:, cols]).astype(BF16).reshape(PER, MAIN, QW)
        send[pl.ds(PER * g, PER), pl.ds(pl.multiple_of(MAIN * q, MAIN), MAIN), :] = block

    def each_partner(g, action):
        for j in range(PER - 1):
            action(PER * g + j)

        @pl.when(g < PARTS - 1)
        def _():
            action(PER * g + PER - 1)

    def dispatch_early(q, total):
        total = take_two(q, total)

        def one_part(g, _):
            main_rows(q, g)
            rows = pl.ds(pl.multiple_of(MAIN * q, MAIN), MAIN)
            each_partner(
                g, lambda o: remote(send.at[o, rows], recv.at[o, rows], d_ssem, d_rsem.at[g], device(o), z)
            )
            return 0

        lax.fori_loop(0, PARTS, one_part, 0)
        return total

    total = lax.fori_loop(0, QUARTERS - 1, dispatch_early, jnp.zeros((TOK, 1), F32))
    total = take_two(QUARTERS - 1, total)
    scale = lax.rsqrt(total * (1.0 / WIDTH) + 1e-05)

    def dispatch_last(g, _):
        main_rows(QUARTERS - 1, g)
        part = iota((16 * PER, TOK), 0) % 16 // 4
        spill = jnp.zeros((16 * PER, QW), F32)
        wide = left_ref[g].astype(F32)
        for q in range(QUARTERS):
            spill += mm(jnp.where(part == q, wide, 0.0).astype(BF16), normed_ref[:, QW * q : QW * q + QW])
        send[pl.ds(PER * g, PER), MAIN * QUARTERS :, :] = spill.astype(BF16).reshape(PER, 16, QW)
        lines = []
        for per in (MAIN, 16):
            want = iota((TOK, PER * per), 1) % (MAIN if per == MAIN else 4) + (0 if per == MAIN else MAIN)
            hit = part_hits(e, g, per, want.astype(F32), slot_ref)
            lines.append(jnp.sum(jnp.where(hit[0] | hit[1], scale, 0.0), axis=0, keepdims=True))
        ssend[g] = jnp.concatenate(
            [lines[0][:, :128], lines[0][:, 128:], lines[1], jnp.zeros((5, 128), F32)], axis=0
        )
        rows = pl.ds(MAIN * (QUARTERS - 1), MAIN + 16)

        def action(o):
            remote(send.at[o, rows], recv.at[o, rows], d_ssem, d_rsem.at[g], device(o), z)
            remote(ssend.at[g], srecv.at[o], s_ssem, s_rsem.at[g], device(o), z)

        each_partner(g, action)

        @pl.when(g == PARTS - 1)
        def _():
            pltpu.make_async_copy(send.at[HOMES - 1], recv.at[HOMES - 1], d_rsem.at[g]).start()
            pltpu.make_async_copy(ssend.at[g], srecv.at[HOMES - 1], s_rsem.at[g]).start()

        return 0

    lax.fori_loop(0, PARTS, dispatch_last, 0)
    for copy in weights:
        copy.wait()
    hot = spare_ref[(e + 16) % 32]

    def expert(g, _):
        await_bytes(recv.at[pl.ds(PER * g, PER)], d_rsem.at[g])
        await_bytes(srecv.at[pl.ds(PER * g, PER)], s_rsem.at[g])
        ffn_group(g, groups, srecv, recv, wg_ref, wu_ref, wd_ref, give, hot)
        each_partner(g, lambda o: remote(give.at[o], ret.at[o], r_ssem, r_rsem.at[g], device(o, -1), z))

        @pl.when(g == PARTS - 1)
        def _():
            pltpu.make_async_copy(give.at[HOMES - 1], ret.at[HOMES - 1], r_rsem.at[g]).start()

        return 0

    lax.fori_loop(0, PARTS, expert, 0)

    def combine(g, _):
        await_bytes(ret.at[pl.ds(PER * g, PER)], r_rsem.at[g])
        left = ret[pl.ds(PER * g, PER), MAIN * QUARTERS :, :].reshape(PER * 16, QW)
        part = iota((TOK, PER * 16), 1) % 16 // 4
        for q in range(QUARTERS):
            main = ret[pl.ds(PER * g, PER), MAIN * q : MAIN * q + MAIN, :].reshape(PER * MAIN, QW)
            moe = mm(wmain_ref[g, 0], main) + mm(wmain_ref[g, 1], main)
            for w in range(2):
                moe += mm(jnp.where(part == q, wleft_ref[g, w].astype(F32), 0.0).astype(BF16), left)
            cut = slice(QW * q, QW * q + QW)
            hid_ref[:, cut] += moe
        return 0

    lax.fori_loop(0, PARTS, combine, 0)
    for i in range(GROUPS):
        out_ref[:, group_cols(groups[i])] = hid_ref[:, 256 * i : 256 * i + 256].astype(BF16)
    await_bytes(rims.at[0], t_ssem.at[0])
    await_bytes(rims.at[1], t_ssem.at[1])
    await_bytes(fsend.at[pl.ds(0, HOMES - 1)], f_ssem)
    await_bytes(csend.at[pl.ds(0, NEAR - 1)], v_ssem)
    await_bytes(csend.at[pl.ds(0, NEAR - 1)], c_ssem)
    await_bytes(srecv.at[pl.ds(0, HOMES - 1)], s_ssem)
    await_bytes(send.at[pl.ds(0, HOMES - 1)], d_ssem)
    await_bytes(send.at[pl.ds(0, HOMES - 1)], r_ssem)


def body(
    resid,
    gate_in,
    gate_short,
    value_short,
    long_filter,
    skip_gain,
    norm_gain,
    expert_ids,
    gate_wts,
    spare_pick,
    w_gate,
    w_up,
    w_down,
):
    vmem, smem, anywhere = (pl.BlockSpec(memory_space=space) for space in (pltpu.VMEM, pltpu.SMEM, pl.ANY))
    dma = pltpu.SemaphoreType.DMA
    message = pltpu.VMEM((HOMES, MSG, QW), BF16)
    pieces = pltpu.VMEM((NEAR, 16, 128), BF16)
    by_group = pltpu.VMEM((GROUPS, HOMES, 16, 128), BF16)
    taps = pltpu.VMEM((HOMES, CH, 128), F32)
    scratch = [
        by_group,
        pieces,
        taps,
        taps,
        pieces,
        by_group,
        pltpu.VMEM((2, 16, WIDTH), BF16),
        pltpu.VMEM((POS, 128), F32),
        pltpu.VMEM((CH, POS), F32),
        pltpu.VMEM((CH, 256, 256), F32),
        pltpu.VMEM((CH, 128, PAD + POS), BF16),
        pltpu.VMEM((256, 256), F32),
        pltpu.VMEM((TOK, WIDTH), F32),
        pltpu.VMEM((TOK, WIDTH), BF16),
        pltpu.VMEM((64, TOK), F32),
        pltpu.VMEM((TOK, 64), BF16),
        pltpu.VMEM((2, TOK, 64), BF16),
        pltpu.VMEM((PARTS, PER * MAIN, TOK), BF16),
        pltpu.VMEM((PARTS, PER * 16, TOK), BF16),
        pltpu.VMEM((PARTS, 2, TOK, PER * MAIN), BF16),
        pltpu.VMEM((PARTS, 2, TOK, PER * 16), BF16),
        message,
        message,
        message,
        message,
        pltpu.VMEM((PARTS, 8, 128), F32),
        pltpu.VMEM((HOMES, 8, 128), F32),
        pltpu.VMEM(w_gate.shape, BF16),
        pltpu.VMEM(w_up.shape, BF16),
        pltpu.VMEM(w_down.shape, BF16),
        pltpu.SemaphoreType.REGULAR,
        dma((3,)),
        dma((2,)),
        dma((2,)),
        dma,
        dma,
        dma,
        dma,
        dma,
        dma((GROUPS,)),
        dma,
        dma((PARTS,)),
        dma,
        dma((PARTS,)),
        dma,
        dma((PARTS,)),
    ]
    return pl.pallas_call(
        layer_kernel,
        out_shape=jax.ShapeDtypeStruct((TOK, WIDTH), BF16),
        in_specs=[smem] * 2 + [vmem] * 9 + [anywhere] * 3,
        out_specs=vmem,
        scratch_shapes=scratch,
        compiler_params=pltpu.CompilerParams(vmem_limit_bytes=VMEM_LIMIT, collective_id=0, has_side_effects=True),
        name="layer",
    )(
        spare_pick,
        skip_gain,
        resid,
        gate_in,
        gate_short,
        value_short,
        long_filter,
        norm_gain.reshape(1, WIDTH),
        expert_ids.T,
        gate_wts.T,
        spare_pick.reshape(1, HOMES),
        w_gate,
        w_up,
        w_down,
    )


def solution(mesh):
    placed = (
        P(("expert", "seq"), None),
        P(("expert", "seq"), None),
        P(),
        P(),
        P("expert", "seq"),
        P("seq"),
        P(),
        P(("expert", "seq"), None),
        P(("expert", "seq"), None),
        P(),
        P("expert", None, None),
        P("expert", None, None),
        P("expert", None, None),
    )
    return jax.shard_map(
        body, mesh=mesh, in_specs=placed, out_specs=P(("expert", "seq"), None), check_vma=False
    )
```

```python
import functools

import jax
import jax.numpy as jnp
from jax import lax
from jax.experimental import pallas as pl
from jax.experimental.pallas import tpu as pltpu
from jax.sharding import PartitionSpec as P

F32, BF16, I32 = jnp.float32, jnp.bfloat16, jnp.int32
VMEM_LIMIT = 60 * 1024 * 1024
TOK = 256
WIDTH = 2048
HOMES = 32
GROUPS = 8
SEQS = 16
BLOCKS = 16
CH = 8
HALVES = 2
SUBS = 16
ROWS = SEQS // HALVES * BLOCKS
PIECES = HALVES * GROUPS
POS = SEQS * TOK
QUARTERS = 4
QW = WIDTH // QUARTERS
MAIN = 32
LEFT = 4
MSG = QUARTERS * (MAIN + LEFT)
CAP = 12
HID = 256
PAD = 128
NEAR = SUBS * GROUPS
PARTS = 4
PER = HOMES // PARTS
MESH = pl.DeviceIdType.MESH


def iota(shape, dim):
    return lax.broadcasted_iota(I32, shape, dim)


def eye(n):
    return (iota((n, n), 0) == iota((n, n), 1)).astype(BF16)


def nt(a, b):
    return lax.dot_general(a, b, (((1,), (1,)), ((), ())), preferred_element_type=F32)


def mm(a, b):
    return jnp.dot(a, b, preferred_element_type=F32)


def short_conv(x, before2, before1, kernel):
    row = iota(x.shape, 0)
    back1 = jnp.where(row == 0, before1, pltpu.roll(x, 1, 0))
    back2 = jnp.where(row == 0, before2, jnp.where(row == 1, before1, pltpu.roll(x, 2, 0)))
    return kernel[0:1] * x + kernel[1:2] * back1 + kernel[2:3] * back2


def group_cols(g):
    return pl.ds(pl.multiple_of(g * 256, 256), 256)


def to_message(block):
    first = block[:, :128].reshape(32, 8, 128)
    second = block[:, 128:].reshape(32, 8, 128)
    return jnp.concatenate([first, second], axis=1).astype(BF16)


def from_message(message):
    wide = message.astype(F32)
    first = wide[:, :8].reshape(128, 128).astype(BF16)
    second = wide[:, 8:].reshape(128, 128).astype(BF16)
    ident = eye(128)
    return jnp.concatenate([nt(ident, first), nt(ident, second)], axis=0)


def partner(order):
    t = (order + 1) * 11 % 32
    return 2 * (t % 2) + t // 2 % 2, 2 * (t // 4 % 2) + t // 8 % 2, t // 16


def ahead(e, offset, sign):
    dx, dy, dc = offset
    x = (e // 8 + 4 + sign * dx) % 4
    y = (e // 2 % 4 + 4 + sign * dy) % 4
    return 8 * x + 2 * y + (e + dc) % 2


def slots(named, rep, axis):
    tri = (iota((TOK, TOK), axis) < iota((TOK, TOK), 1 - axis)).astype(BF16)
    if axis == 0:
        rank = mm(named.astype(BF16), tri)
    else:
        rank = mm(tri, named.astype(BF16))
    kept = (named > 0) & ((rank < CAP) | ((rank < 2 * CAP) & (rep > 0)))
    return jnp.where(kept, jnp.where(rep > 0, rank, rank + 2 * CAP), -1.0)


def prepare_routing(spare_ref, idst_ref, wtst_ref, slott_ref, slot_ref, weight_ref):
    expert, index = iota((64, HOMES), 0), iota((64, HOMES), 1)
    picked = jnp.where(index == (expert // 2 + 16) % 32, spare_ref[...], 0)
    rep = jnp.sum(picked.astype(F32), axis=1, keepdims=True) == (iota((64, 1), 0) % 2).astype(F32)
    named = jnp.zeros((64, TOK), F32)
    weight = jnp.zeros((64, TOK), F32)
    for k in range(4):
        hit = idst_ref[k : k + 1, :] == iota((64, TOK), 0)
        named += hit.astype(F32)
        weight += jnp.where(hit, wtst_ref[k : k + 1, :], 0.0)
    slot = slots(named, rep.astype(F32), 0)
    slott_ref[...] = slot
    ident = eye(TOK)
    slot_ref[...] = nt(ident, slot.astype(BF16)).astype(BF16)
    high = weight.astype(BF16)
    weight_ref[0] = nt(ident, high).astype(BF16)
    weight_ref[1] = nt(ident, (weight - high.astype(F32)).astype(BF16)).astype(BF16)


def part_picks(e, g, per):
    shape = (64, PER * per)
    home = ahead(e, partner(PER * g + iota(shape, 1) // per), 1)
    return [(iota(shape, 0) == 2 * home + odd).astype(BF16) for odd in range(2)]


def part_hits(e, g, per, want, slot_ref):
    return [mm(slot_ref[...], pick) == want for pick in part_picks(e, g, per)]


def part_weights(e, g, per, want, slot_ref, weight_ref):
    high = low = jnp.zeros((TOK, PER * per), F32)
    for pick in part_picks(e, g, per):
        hit = mm(slot_ref[...], pick) == want
        high = high + jnp.where(hit, mm(weight_ref[0], pick), 0.0)
        low = low + jnp.where(hit, mm(weight_ref[1], pick), 0.0)
    return high.astype(BF16), low.astype(BF16)


def build_bank(row, bank_ref):
    wide = jnp.concatenate([jnp.broadcast_to(row, (8, POS)), jnp.zeros((8, PAD), F32)], axis=1)
    base = pltpu.roll(wide, 0, 1, stride=1, stride_axis=0)
    for a in range(8):
        upper = pltpu.roll(base, 16 * a, 1) if a else base
        lower = pltpu.roll(base, 16 * a + 8, 1)
        both = jnp.concatenate([upper, lower], axis=0)[:, :POS].astype(BF16)
        bank_ref[16 * a : 16 * a + 16, PAD:] = both


def arrival(i):
    return jnp.where(i % 2 == 1, (i + 1) // 2, GROUPS - i // 2) % GROUPS


def silu_mul(gate, up):
    return gate / (1.0 + jnp.exp(-gate)) * up


def scale_columns(g, scales, lanes_of, per):
    cols = []
    for j in range(PER):
        sub, lane, rows = lanes_of(j)
        line = scales[PER * g + j, sub : sub + 1, :]
        hit = iota((per, 128), 1) == lane + iota((per, 128), 0)
        cols.append(jnp.sum(jnp.where(hit, line, 0.0), axis=1, keepdims=True))
    return jnp.concatenate(cols, axis=0)


def ffn_group(g, rows_of, scales, recv_ref, wg_ref, wu_ref, wd_ref, out_ref, hot):
    cold = 1 - hot
    n = PER
    src = pl.ds(g * PER, n)
    rows = 16 * n
    zero = functools.partial(jnp.zeros, (rows, HID), F32)
    ga, ua, gb, ub, gc, uc, gl, ul = (zero() for _ in range(8))
    part = iota((rows, HID), 0) % 16 // 4
    for i in range(GROUPS):
        q = i // 2
        lanes = slice(256 * (i % 2), 256 * (i % 2) + 256)
        xa = recv_ref[src, MAIN * q : MAIN * q + 16, lanes].reshape(rows, 256)
        xb = recv_ref[src, MAIN * q + 16 : MAIN * q + 32, lanes].reshape(rows, 256)
        left = recv_ref[src, MAIN * QUARTERS :, lanes].reshape(rows, 256)
        both = jnp.concatenate([xa, xb], axis=0)
        gh, uh = mm(both, rows_of(wg_ref, hot, i)), mm(both, rows_of(wu_ref, hot, i))
        ga, ua, gb, ub = ga + gh[:rows], ua + uh[:rows], gb + gh[rows:], ub + uh[rows:]
        both = jnp.concatenate([xb, left], axis=0)
        gh, uh = mm(both, rows_of(wg_ref, cold, i)), mm(both, rows_of(wu_ref, cold, i))
        gc, uc = gc + gh[:rows], uc + uh[:rows]
        gl = gl + jnp.where(part == q, gh[rows:], 0.0)
        ul = ul + jnp.where(part == q, uh[rows:], 0.0)

    def over_quarters(acc):
        acc = acc.reshape(n, 16, HID)
        acc = acc[:, :8] + acc[:, 8:]
        acc = acc.reshape(8 * n, HID)
        low = iota(acc.shape, 0) % 8 < 4
        other = jnp.where(low, pltpu.roll(acc, 8 * n - 4, 0), pltpu.roll(acc, 4, 0))
        acc = (acc + other).reshape(n, 8, HID)
        return jnp.concatenate([acc, acc], axis=1).reshape(rows, HID)

    sa = scale_columns(g, scales, lambda j: (j // 4, 32 * (j % 4), 16), 16)
    sb = scale_columns(g, scales, lambda j: (j // 4, 32 * (j % 4) + 16, 16), 16)
    sl = scale_columns(g, scales, lambda j: (2, 16 * j, 16), 16)
    is_hot = iota((rows, HID), 0) % 16 < 8
    act_a = silu_mul(ga * sa, ua * sa).astype(BF16)
    act_b = silu_mul(jnp.where(is_hot, gb, gc) * sb, jnp.where(is_hot, ub, uc) * sb)
    act_bh = jnp.where(is_hot, act_b, 0.0).astype(BF16)
    act_bc = jnp.where(is_hot, 0.0, act_b).astype(BF16)
    act_l = silu_mul(over_quarters(gl) * sl, over_quarters(ul) * sl).astype(BF16)
    hot_in = jnp.concatenate([act_a, act_bh], axis=0)
    cold_in = jnp.concatenate([act_bc, act_l], axis=0)
    part = iota((rows, 256), 0) % 16 // 4
    spill = [jnp.zeros((rows, 256), F32)] * 2
    for i in range(GROUPS):
        q = i // 2
        lanes = slice(256 * (i % 2), 256 * (i % 2) + 256)
        oh = nt(hot_in, rows_of(wd_ref, hot, i))
        oc = nt(cold_in, rows_of(wd_ref, cold, i))
        out_ref[src, MAIN * q : MAIN * q + 16, lanes] = oh[:rows].astype(BF16).reshape(n, 16, 256)
        out_ref[src, MAIN * q + 16 : MAIN * q + 32, lanes] = (oh[rows:] + oc[:rows]).astype(BF16).reshape(n, 16, 256)
        spill[i % 2] = jnp.where(part == q, oc[rows:], spill[i % 2])
    out_ref[src, MAIN * QUARTERS :, :] = jnp.concatenate(spill, axis=1).astype(BF16).reshape(n, 16, QW)


def layer_kernel(
    spare_ref, skip_ref, resid_ref, gate_in_ref, gate_kern_ref, value_kern_ref, filt_ref, gain_ref, idst_ref, wtst_ref,
    row_ref, wg_hbm, wu_hbm, wd_hbm, out_ref,
    vsend, vrecv, fsend, frecv, csend, crecv, tail_send, tail_recv, rim_ref, wide_ref, hrow_ref, x_ref, bank_ref, acc_ref,
    hid_ref, normed_ref, slott_ref, slot_ref, weight_ref, sel_ref, left_ref, wmain_ref, wleft_ref,
    send, recv, give, ret, ssend, srecv, wg_ref, wu_ref, wd_ref,
    b_sem, w_sem, t_ssem, t_rsem, f_ssem, f_rsem, v_ssem, v_rsem, c_ssem, c_rsem, s_ssem, s_rsem, d_ssem, d_rsem, r_ssem, r_rsem,
):
    e, z = lax.axis_index("expert"), lax.axis_index("seq")

    sub, side = e // 8 * 4 + e % 4, e // 4 % 2

    def device(order, sign=1):
        return ahead(e, partner(order), sign)

    def remote(source, sink, ssem, rsem, expert, seq):
        pltpu.make_async_remote_copy(
            src_ref=source, dst_ref=sink, send_sem=ssem, recv_sem=rsem, device_id=(expert, seq), device_id_type=MESH
        ).start()

    def await_bytes(ref, sem):
        pltpu.make_async_copy(ref, ref, sem).wait()

    barrier = pltpu.get_barrier_semaphore()
    before = ((e + HOMES - 1 + (z + GROUPS - 1) // GROUPS) % HOMES, (z + GROUPS - 1) % GROUPS)
    after = ((e + (z + 1) // GROUPS) % HOMES, (z + 1) % GROUPS)
    pl.semaphore_signal(barrier, inc=1, device_id=before, device_id_type=MESH)

    def greet_line(dz, _):
        pl.semaphore_signal(barrier, inc=1, device_id=(e, (z + dz) % GROUPS), device_id_type=MESH)
        return 0

    def greet_plane(order, _):
        pl.semaphore_signal(barrier, inc=1, device_id=(device(order), z), device_id_type=MESH)
        return 0

    lax.fori_loop(1, GROUPS, greet_line, 0)
    lax.fori_loop(0, HOMES - 1, greet_plane, 0)
    weights = [
        pltpu.make_async_copy(hbm, vmem, w_sem.at[i])
        for i, (hbm, vmem) in enumerate(((wg_hbm, wg_ref), (wu_hbm, wu_ref), (wd_hbm, wd_ref)))
    ]
    for copy in weights:
        copy.start()
    ident = eye(256)
    flipped = nt(ident, filt_ref[...]).reshape(HALVES, SUBS, CH, 128)
    for h in range(HALVES):
        fsend[:, h] = flipped[h]
    tail = jnp.concatenate(
        [ref[TOK - 16 :, :].astype(F32)[14:16] for ref in (gate_in_ref, resid_ref)], axis=0
    )
    tail_send[...] = jnp.concatenate([tail[:, QW * q : QW * q + QW] for q in range(QUARTERS)], axis=0).astype(BF16)
    pl.semaphore_wait(barrier, GROUPS - 1 + HOMES - 1 + 1)

    remote(tail_send, tail_recv, t_ssem, t_rsem, *after)

    def greet_again(dz, _):
        pl.semaphore_signal(b_sem, inc=1, device_id=(e, (z + dz) % GROUPS), device_id_type=MESH)
        return 0

    lax.fori_loop(1, GROUPS, greet_again, 0)

    def send_filter(order, _):
        target = device(order)
        remote(fsend.at[target // 8 * 4 + target % 4], frecv.at[e], f_ssem, f_rsem, target, z)
        return 0

    lax.fori_loop(0, HOMES - 1, send_filter, 0)
    frecv[e] = fsend[sub]
    at_start = (z == 0) & (e % 2 == 0)

    def branch(ref, which, cols, kernel):
        return short_conv(
            ref[:, cols].astype(F32), rim_ref[2 * which : 2 * which + 1, cols], rim_ref[2 * which + 1 : 2 * which + 2, cols], kernel
        )

    def mate(t):
        target = (e // 8 + t // 4) % 4 * 8 + side * 4 + (e // 2 + t // 2) % 2 * 2 + (e + t) % 2
        return target, target // 8 * 4 + target % 4

    def place_of(expert, seq):
        return (expert % 2 * GROUPS + seq) * (SEQS // HALVES) + expert // 8 * 2 + expert // 2 % 2

    await_bytes(tail_recv, t_rsem)
    tail = tail_recv[...].astype(F32)
    for q in range(QUARTERS):
        rim_ref[:, QW * q : QW * q + QW] = jnp.where(at_start, 0.0, tail[4 * q : 4 * q + 4])
    row = place_of(e, z)

    def send_values(h, there):
        def one(t, _):
            target, share = mate(t)
            remote(vsend.at[there, h * SUBS + share], vrecv.at[h, row], v_ssem, v_rsem.at[h], target, there)
            return 0

        lax.fori_loop(1, SUBS, one, 0)

        @pl.when(there != z)
        def _():
            remote(vsend.at[there, h * SUBS + sub], vrecv.at[h, row], v_ssem, v_rsem.at[h], e, there)

    def make_values(r, _):
        there = (z + 3 * r + 4) % GROUPS
        cols = group_cols(there)
        values = branch(resid_ref, 1, cols, value_kern_ref[:, cols]).astype(BF16)
        vsend[there] = to_message(nt(ident, values))

        @pl.when(r == 0)
        def _():
            pl.semaphore_wait(b_sem, GROUPS - 1)

        send_values(0, there)
        return 0

    lax.fori_loop(0, GROUPS, make_values, 0)

    def rest_of_values(r, _):
        send_values(1, (z + 3 * r + 4) % GROUPS)
        return 0

    lax.fori_loop(0, GROUPS, rest_of_values, 0)
    for h in range(HALVES):
        vrecv[h, row] = vsend[z, h * SUBS + sub]

    await_bytes(frecv.at[pl.ds(0, HOMES - 1)], f_rsem)
    for d in range(HOMES):
        for h in range(HALVES):
            hrow_ref[CH * h : CH * h + CH, 128 * d : 128 * d + 128] = frecv[d, h]
    bank_ref[:, :, :PAD] = jnp.zeros((CH, 128, PAD), BF16)

    def make_bank(h):
        def bank(c, _):
            build_bank(hrow_ref[pl.ds(CH * h + c, 1), :], bank_ref.at[c])
            return 0

        lax.fori_loop(0, CH, bank, 0)

    make_bank(0)
    prepare_routing(row_ref, idst_ref, wtst_ref, slott_ref, slot_ref, weight_ref)

    def select(g, _):
        sel = []
        left = []
        for j in range(PER):
            home = device(PER * g + j)
            even = slott_ref[pl.ds(2 * home, 1), :]
            odd = slott_ref[pl.ds(2 * home + 1, 1), :]
            r = iota((MAIN, TOK), 0).astype(F32)
            sel.append(((even == r) | (odd == r)).astype(BF16))
            r = (iota((16, TOK), 0) % 4 + MAIN).astype(F32)
            left.append(((even == r) | (odd == r)).astype(BF16))
        sel_ref[g] = jnp.concatenate(sel, axis=0)
        left_ref[g] = jnp.concatenate(left, axis=0)
        want = (iota((TOK, PER * MAIN), 1) % MAIN).astype(F32)
        wmain_ref[g, 0], wmain_ref[g, 1] = part_weights(e, g, MAIN, want, slot_ref, weight_ref)
        want = (iota((TOK, PER * 16), 1) % 4 + MAIN).astype(F32)
        wleft_ref[g, 0], wleft_ref[g, 1] = part_weights(e, g, 16, want, slot_ref, weight_ref)
        return 0

    lax.fori_loop(0, PARTS, select, 0)
    def convolve(h):
        await_bytes(vrecv.at[h, pl.ds(0, NEAR - 1)], v_rsem.at[h])
        for i in range(8):
            wide_ref[256 * i : 256 * i + 256] = vrecv[h, 16 * i : 16 * i + 16].astype(F32).reshape(256, 128)
        for c in range(CH):
            for half in range(2):
                x_ref[c, :, 128 * half : 128 * half + 128] = wide_ref[pl.ds(8 * half + c, ROWS, stride=16), :]

        def conv(c, _):
            acc_ref[...] = x_ref[c] * skip_ref[h * SUBS * CH + sub * CH + c]
            for k in range(BLOCKS):
                upper = bank_ref[c, :, PAD + 256 * k : PAD + 256 * k + 256]
                lower = bank_ref[c, :, 256 * k : 256 * k + 256]
                lhs = x_ref[c, : ROWS - 8 * k, :].astype(BF16)
                acc_ref[8 * k :, :] += mm(lhs, jnp.concatenate([upper, lower], axis=0))
            x_ref[c] = acc_ref[...]
            return 0

        lax.fori_loop(0, CH, conv, 0)
        for c in range(CH):
            for half in range(2):
                wide_ref[pl.ds(8 * half + c, ROWS, stride=16), :] = x_ref[c, :, 128 * half : 128 * half + 128]
        for i in range(8):
            csend[h, 16 * i : 16 * i + 16] = wide_ref[256 * i : 256 * i + 256].reshape(16, 16, 128).astype(BF16)

        def send_back(i, _):
            there = (z + arrival(i)) % GROUPS
            sem = c_rsem.at[h * GROUPS + i]

            def send_plane(t, _):
                target, _ = mate(t)
                remote(csend.at[h, place_of(target, there)], crecv.at[h, i, sub], c_ssem, sem, target, there)
                return 0

            lax.fori_loop(1, SUBS, send_plane, 0)

            @pl.when(there != z)
            def _():
                remote(csend.at[h, place_of(e, there)], crecv.at[h, i, sub], c_ssem, sem, e, there)

            return 0

        lax.fori_loop(0, GROUPS, send_back, 0)
        pltpu.make_async_copy(csend.at[h, row], crecv.at[h, 0, sub], c_rsem.at[h * GROUPS]).start()

    convolve(0)
    make_bank(1)

    def piece_cols(p):
        group = (z + GROUPS - arrival(p % GROUPS)) % GROUPS
        return pl.ds(pl.multiple_of(group * 256 + p // GROUPS * 128, 128), 128)

    def rows_of(ref, which, i):
        return jnp.concatenate([ref[which, piece_cols(jnp.int32(p)), :] for p in (2 * i, 2 * i + 1)], axis=0)

    def take(p, total):
        h, i = p // GROUPS, p % GROUPS
        await_bytes(crecv.at[h, i], c_rsem.at[p])
        cols, mine = piece_cols(p), pl.ds(pl.multiple_of(128 * p, 128), 128)
        gated = branch(gate_in_ref, 0, cols, gate_kern_ref[:, cols])
        hidden = resid_ref[:, cols].astype(F32) + gated * from_message(crecv[h, i])
        hid_ref[:, mine] = hidden
        normed_ref[:, mine] = (hidden * gain_ref[:, cols]).astype(BF16)
        return total + jnp.sum(hidden * hidden, axis=1, keepdims=True)

    def take_quarter(q, total):
        return lax.fori_loop(4 * q, 4 * q + 4, take, total)

    def main_rows(q, g):
        cols = pl.ds(pl.multiple_of(QW * q, QW), QW)
        block = mm(sel_ref[g], normed_ref[:, cols]).astype(BF16).reshape(PER, MAIN, QW)
        send[pl.ds(PER * g, PER), pl.ds(pl.multiple_of(MAIN * q, MAIN), MAIN), :] = block

    def each_partner(g, action):
        for j in range(PER - 1):
            action(PER * g + j)

        @pl.when(g < PARTS - 1)
        def _():
            action(PER * g + PER - 1)

    def dispatch_early(q, total):
        total = take_quarter(q, total)

        def one_part(g, _):
            main_rows(q, g)
            rows = pl.ds(pl.multiple_of(MAIN * q, MAIN), MAIN)
            each_partner(
                g, lambda o: remote(send.at[o, rows], recv.at[o, rows], d_ssem, d_rsem.at[g], device(o), z)
            )
            return 0

        lax.fori_loop(0, PARTS, one_part, 0)
        return total

    total = dispatch_early(jnp.int32(0), jnp.zeros((TOK, 1), F32))
    convolve(1)
    total = lax.fori_loop(1, QUARTERS - 1, dispatch_early, total)
    total = take_quarter(QUARTERS - 1, total)
    scale = lax.rsqrt(total * (1.0 / WIDTH) + 1e-05)

    def dispatch_last(g, _):
        main_rows(QUARTERS - 1, g)
        part = iota((16 * PER, TOK), 0) % 16 // 4
        spill = jnp.zeros((16 * PER, QW), F32)
        wide = left_ref[g].astype(F32)
        for q in range(QUARTERS):
            spill += mm(jnp.where(part == q, wide, 0.0).astype(BF16), normed_ref[:, QW * q : QW * q + QW])
        send[pl.ds(PER * g, PER), MAIN * QUARTERS :, :] = spill.astype(BF16).reshape(PER, 16, QW)
        lines = []
        for per in (MAIN, 16):
            want = iota((TOK, PER * per), 1) % (MAIN if per == MAIN else 4) + (0 if per == MAIN else MAIN)
            hit = part_hits(e, g, per, want.astype(F32), slot_ref)
            lines.append(jnp.sum(jnp.where(hit[0] | hit[1], scale, 0.0), axis=0, keepdims=True))
        ssend[g] = jnp.concatenate(
            [lines[0][:, :128], lines[0][:, 128:], lines[1], jnp.zeros((5, 128), F32)], axis=0
        )
        rows = pl.ds(MAIN * (QUARTERS - 1), MAIN + 16)

        def action(o):
            remote(send.at[o, rows], recv.at[o, rows], d_ssem, d_rsem.at[g], device(o), z)
            remote(ssend.at[g], srecv.at[o], s_ssem, s_rsem.at[g], device(o), z)

        each_partner(g, action)

        @pl.when(g == PARTS - 1)
        def _():
            pltpu.make_async_copy(send.at[HOMES - 1], recv.at[HOMES - 1], d_rsem.at[g]).start()
            pltpu.make_async_copy(ssend.at[g], srecv.at[HOMES - 1], s_rsem.at[g]).start()

        return 0

    lax.fori_loop(0, PARTS, dispatch_last, 0)
    for copy in weights:
        copy.wait()
    hot = spare_ref[(e + 16) % 32]

    def expert(g, _):
        await_bytes(recv.at[pl.ds(PER * g, PER)], d_rsem.at[g])
        await_bytes(srecv.at[pl.ds(PER * g, PER)], s_rsem.at[g])
        ffn_group(g, rows_of, srecv, recv, wg_ref, wu_ref, wd_ref, give, hot)
        each_partner(g, lambda o: remote(give.at[o], ret.at[o], r_ssem, r_rsem.at[g], device(o, -1), z))

        @pl.when(g == PARTS - 1)
        def _():
            pltpu.make_async_copy(give.at[HOMES - 1], ret.at[HOMES - 1], r_rsem.at[g]).start()

        return 0

    lax.fori_loop(0, PARTS, expert, 0)

    def combine(g, _):
        await_bytes(ret.at[pl.ds(PER * g, PER)], r_rsem.at[g])
        left = ret[pl.ds(PER * g, PER), MAIN * QUARTERS :, :].reshape(PER * 16, QW)
        part = iota((TOK, PER * 16), 1) % 16 // 4
        for q in range(QUARTERS):
            main = ret[pl.ds(PER * g, PER), MAIN * q : MAIN * q + MAIN, :].reshape(PER * MAIN, QW)
            moe = mm(wmain_ref[g, 0], main) + mm(wmain_ref[g, 1], main)
            for w in range(2):
                moe += mm(jnp.where(part == q, wleft_ref[g, w].astype(F32), 0.0).astype(BF16), left)
            cut = slice(QW * q, QW * q + QW)
            hid_ref[:, cut] += moe
        return 0

    lax.fori_loop(0, PARTS, combine, 0)
    for p in range(PIECES):
        out_ref[:, piece_cols(jnp.int32(p))] = hid_ref[:, 128 * p : 128 * p + 128].astype(BF16)
    await_bytes(tail_send, t_ssem)
    await_bytes(frecv.at[pl.ds(0, HOMES - 1)], f_ssem)
    for sem in (v_ssem, c_ssem):
        await_bytes(csend.at[:, pl.ds(0, NEAR - 1)], sem)
    await_bytes(srecv.at[pl.ds(0, HOMES - 1)], s_ssem)
    await_bytes(send.at[pl.ds(0, HOMES - 1)], d_ssem)
    await_bytes(send.at[pl.ds(0, HOMES - 1)], r_ssem)


def body(
    resid,
    gate_in,
    gate_short,
    value_short,
    long_filter,
    skip_gain,
    norm_gain,
    expert_ids,
    gate_wts,
    spare_pick,
    w_gate,
    w_up,
    w_down,
):
    vmem, smem, anywhere = (pl.BlockSpec(memory_space=space) for space in (pltpu.VMEM, pltpu.SMEM, pl.ANY))
    dma = pltpu.SemaphoreType.DMA
    message = pltpu.VMEM((HOMES, MSG, QW), BF16)
    by_row = pltpu.VMEM((HALVES, NEAR, 16, 128), BF16)
    scratch = [
        pltpu.VMEM((GROUPS, HOMES, 16, 128), BF16),
        by_row,
        pltpu.VMEM((SUBS, HALVES, CH, 128), F32),
        pltpu.VMEM((HOMES, HALVES, CH, 128), F32),
        by_row,
        pltpu.VMEM((HALVES, GROUPS, SUBS, 16, 128), BF16),
        pltpu.VMEM((16, QW), BF16),
        pltpu.VMEM((16, QW), BF16),
        pltpu.VMEM((4, WIDTH), F32),
        pltpu.VMEM((ROWS * 16, 128), F32),
        pltpu.VMEM((HALVES * CH, POS), F32),
        pltpu.VMEM((CH, ROWS, 256), F32),
        pltpu.VMEM((CH, 128, PAD + POS), BF16),
        pltpu.VMEM((ROWS, 256), F32),
        pltpu.VMEM((TOK, WIDTH), F32),
        pltpu.VMEM((TOK, WIDTH), BF16),
        pltpu.VMEM((64, TOK), F32),
        pltpu.VMEM((TOK, 64), BF16),
        pltpu.VMEM((2, TOK, 64), BF16),
        pltpu.VMEM((PARTS, PER * MAIN, TOK), BF16),
        pltpu.VMEM((PARTS, PER * 16, TOK), BF16),
        pltpu.VMEM((PARTS, 2, TOK, PER * MAIN), BF16),
        pltpu.VMEM((PARTS, 2, TOK, PER * 16), BF16),
        message,
        message,
        message,
        message,
        pltpu.VMEM((PARTS, 8, 128), F32),
        pltpu.VMEM((HOMES, 8, 128), F32),
        pltpu.VMEM(w_gate.shape, BF16),
        pltpu.VMEM(w_up.shape, BF16),
        pltpu.VMEM(w_down.shape, BF16),
        pltpu.SemaphoreType.REGULAR,
        dma((3,)),
        dma,
        dma,
        dma,
        dma,
        dma,
        dma((HALVES,)),
        dma,
        dma((PIECES,)),
        dma,
        dma((PARTS,)),
        dma,
        dma((PARTS,)),
        dma,
        dma((PARTS,)),
    ]
    return pl.pallas_call(
        layer_kernel,
        out_shape=jax.ShapeDtypeStruct((TOK, WIDTH), BF16),
        in_specs=[smem] * 2 + [vmem] * 9 + [anywhere] * 3,
        out_specs=vmem,
        scratch_shapes=scratch,
        compiler_params=pltpu.CompilerParams(vmem_limit_bytes=VMEM_LIMIT, collective_id=0, has_side_effects=True),
        name="layer",
    )(
        spare_pick,
        skip_gain,
        resid,
        gate_in,
        gate_short,
        value_short,
        long_filter,
        norm_gain.reshape(1, WIDTH),
        expert_ids.T,
        gate_wts.T,
        spare_pick.reshape(1, HOMES),
        w_gate,
        w_up,
        w_down,
    )


def solution(mesh):
    placed = (
        P(("expert", "seq"), None),
        P(("expert", "seq"), None),
        P(),
        P(),
        P("expert", "seq"),
        P("seq"),
        P(),
        P(("expert", "seq"), None),
        P(("expert", "seq"), None),
        P(),
        P("expert", None, None),
        P("expert", None, None),
        P("expert", None, None),
    )
    return jax.shard_map(
        body, mesh=mesh, in_specs=placed, out_specs=P(("expert", "seq"), None), check_vma=False
    )
```

```python
import functools

import jax
import jax.numpy as jnp
from jax import lax
from jax.experimental import pallas as pl
from jax.experimental.pallas import tpu as pltpu
from jax.sharding import PartitionSpec as P

F32, BF16, I32 = jnp.float32, jnp.bfloat16, jnp.int32
VMEM_LIMIT = 60 * 1024 * 1024
TOK = 256
WIDTH = 2048
HOMES = 32
GROUPS = 8
SEQS = 16
BLOCKS = 16
CH = 8
HALVES = 2
SUBS = 16
ROWS = SEQS // HALVES * BLOCKS
PIECES = HALVES * GROUPS
POS = SEQS * TOK
QUARTERS = 4
QW = WIDTH // QUARTERS
MAIN = 32
LEFT = 4
MSG = QUARTERS * (MAIN + LEFT)
CAP = 12
HID = 256
PAD = 128
NEAR = SUBS * GROUPS
PARTS = 4
PER = HOMES // PARTS
MESH = pl.DeviceIdType.MESH


def iota(shape, dim):
    return lax.broadcasted_iota(I32, shape, dim)


def eye(n):
    return (iota((n, n), 0) == iota((n, n), 1)).astype(BF16)


def nt(a, b):
    return lax.dot_general(a, b, (((1,), (1,)), ((), ())), preferred_element_type=F32)


def mm(a, b):
    return jnp.dot(a, b, preferred_element_type=F32)


def short_conv(x, before2, before1, kernel):
    row = iota(x.shape, 0)
    back1 = jnp.where(row == 0, before1, pltpu.roll(x, 1, 0))
    back2 = jnp.where(row == 0, before2, jnp.where(row == 1, before1, pltpu.roll(x, 2, 0)))
    return kernel[0:1] * x + kernel[1:2] * back1 + kernel[2:3] * back2


def group_cols(g):
    return pl.ds(pl.multiple_of(g * 256, 256), 256)


def to_message(block):
    first = block[:, :128].reshape(32, 8, 128)
    second = block[:, 128:].reshape(32, 8, 128)
    return jnp.concatenate([first, second], axis=1).astype(BF16)


def from_message(message):
    wide = message.astype(F32)
    first = wide[:, :8].reshape(128, 128).astype(BF16)
    second = wide[:, 8:].reshape(128, 128).astype(BF16)
    ident = eye(128)
    return jnp.concatenate([nt(ident, first), nt(ident, second)], axis=0)


def partner(order):
    t = (order + 1) * 15 % 32
    return 2 * (t % 2) + t // 2 % 2, 2 * (t // 16) + t // 4 % 2, t // 8 % 2


def ahead(e, offset, sign):
    dx, dy, dc = offset
    x = (e // 8 + 4 + sign * dx) % 4
    y = (e // 2 % 4 + 4 + sign * dy) % 4
    return 8 * x + 2 * y + (e + dc) % 2


def slots(named, rep, axis):
    tri = (iota((TOK, TOK), axis) < iota((TOK, TOK), 1 - axis)).astype(BF16)
    if axis == 0:
        rank = mm(named.astype(BF16), tri)
    else:
        rank = mm(tri, named.astype(BF16))
    kept = (named > 0) & ((rank < CAP) | ((rank < 2 * CAP) & (rep > 0)))
    return jnp.where(kept, jnp.where(rep > 0, rank, rank + 2 * CAP), -1.0)


def prepare_routing(spare_ref, idst_ref, wtst_ref, slott_ref, slot_ref, weight_ref):
    expert, index = iota((64, HOMES), 0), iota((64, HOMES), 1)
    picked = jnp.where(index == (expert // 2 + 16) % 32, spare_ref[...], 0)
    rep = jnp.sum(picked.astype(F32), axis=1, keepdims=True) == (iota((64, 1), 0) % 2).astype(F32)
    named = jnp.zeros((64, TOK), F32)
    weight = jnp.zeros((64, TOK), F32)
    for k in range(4):
        hit = idst_ref[k : k + 1, :] == iota((64, TOK), 0)
        named += hit.astype(F32)
        weight += jnp.where(hit, wtst_ref[k : k + 1, :], 0.0)
    slot = slots(named, rep.astype(F32), 0)
    slott_ref[...] = slot
    ident = eye(TOK)
    slot_ref[...] = nt(ident, slot.astype(BF16)).astype(BF16)
    high = weight.astype(BF16)
    weight_ref[0] = nt(ident, high).astype(BF16)
    weight_ref[1] = nt(ident, (weight - high.astype(F32)).astype(BF16)).astype(BF16)


def part_picks(e, g, per):
    shape = (64, PER * per)
    home = ahead(e, partner(PER * g + iota(shape, 1) // per), 1)
    return [(iota(shape, 0) == 2 * home + odd).astype(BF16) for odd in range(2)]


def part_hits(e, g, per, want, slot_ref):
    return [mm(slot_ref[...], pick) == want for pick in part_picks(e, g, per)]


def part_weights(e, g, per, want, slot_ref, weight_ref):
    high = low = jnp.zeros((TOK, PER * per), F32)
    for pick in part_picks(e, g, per):
        hit = mm(slot_ref[...], pick) == want
        high = high + jnp.where(hit, mm(weight_ref[0], pick), 0.0)
        low = low + jnp.where(hit, mm(weight_ref[1], pick), 0.0)
    return high.astype(BF16), low.astype(BF16)


def build_bank(row, bank_ref):
    wide = jnp.concatenate([jnp.broadcast_to(row, (8, POS)), jnp.zeros((8, PAD), F32)], axis=1)
    base = pltpu.roll(wide, 0, 1, stride=1, stride_axis=0)
    for a in range(8):
        upper = pltpu.roll(base, 16 * a, 1) if a else base
        lower = pltpu.roll(base, 16 * a + 8, 1)
        both = jnp.concatenate([upper, lower], axis=0)[:, :POS].astype(BF16)
        bank_ref[16 * a : 16 * a + 16, PAD:] = both


def arrival(i):
    return jnp.where(i % 2 == 1, (i + 1) // 2, GROUPS - i // 2) % GROUPS


def silu_mul(gate, up):
    return gate / (1.0 + jnp.exp(-gate)) * up


def scale_columns(g, scales, lanes_of, per):
    cols = []
    for j in range(PER):
        sub, lane, rows = lanes_of(j)
        line = scales[PER * g + j, sub : sub + 1, :]
        hit = iota((per, 128), 1) == lane + iota((per, 128), 0)
        cols.append(jnp.sum(jnp.where(hit, line, 0.0), axis=1, keepdims=True))
    return jnp.concatenate(cols, axis=0)


def ffn_group(g, rows_of, scales, recv_ref, wg_ref, wu_ref, wd_ref, out_ref, hot):
    cold = 1 - hot
    n = PER
    src = pl.ds(g * PER, n)
    rows = 16 * n
    zero = functools.partial(jnp.zeros, (rows, HID), F32)
    ga, ua, gb, ub, gc, uc, gl, ul = (zero() for _ in range(8))
    part = iota((rows, HID), 0) % 16 // 4
    for i in range(GROUPS):
        q = i // 2
        lanes = slice(256 * (i % 2), 256 * (i % 2) + 256)
        xa = recv_ref[src, MAIN * q : MAIN * q + 16, lanes].reshape(rows, 256)
        xb = recv_ref[src, MAIN * q + 16 : MAIN * q + 32, lanes].reshape(rows, 256)
        left = recv_ref[src, MAIN * QUARTERS :, lanes].reshape(rows, 256)
        both = jnp.concatenate([xa, xb], axis=0)
        gh, uh = mm(both, rows_of(wg_ref, hot, i)), mm(both, rows_of(wu_ref, hot, i))
        ga, ua, gb, ub = ga + gh[:rows], ua + uh[:rows], gb + gh[rows:], ub + uh[rows:]
        both = jnp.concatenate([xb, left], axis=0)
        gh, uh = mm(both, rows_of(wg_ref, cold, i)), mm(both, rows_of(wu_ref, cold, i))
        gc, uc = gc + gh[:rows], uc + uh[:rows]
        gl = gl + jnp.where(part == q, gh[rows:], 0.0)
        ul = ul + jnp.where(part == q, uh[rows:], 0.0)

    def over_quarters(acc):
        acc = acc.reshape(n, 16, HID)
        acc = acc[:, :8] + acc[:, 8:]
        acc = acc.reshape(8 * n, HID)
        low = iota(acc.shape, 0) % 8 < 4
        other = jnp.where(low, pltpu.roll(acc, 8 * n - 4, 0), pltpu.roll(acc, 4, 0))
        acc = (acc + other).reshape(n, 8, HID)
        return jnp.concatenate([acc, acc], axis=1).reshape(rows, HID)

    sa = scale_columns(g, scales, lambda j: (j // 4, 32 * (j % 4), 16), 16)
    sb = scale_columns(g, scales, lambda j: (j // 4, 32 * (j % 4) + 16, 16), 16)
    sl = scale_columns(g, scales, lambda j: (2, 16 * j, 16), 16)
    is_hot = iota((rows, HID), 0) % 16 < 8
    act_a = silu_mul(ga * sa, ua * sa).astype(BF16)
    act_b = silu_mul(jnp.where(is_hot, gb, gc) * sb, jnp.where(is_hot, ub, uc) * sb)
    act_bh = jnp.where(is_hot, act_b, 0.0).astype(BF16)
    act_bc = jnp.where(is_hot, 0.0, act_b).astype(BF16)
    act_l = silu_mul(over_quarters(gl) * sl, over_quarters(ul) * sl).astype(BF16)
    hot_in = jnp.concatenate([act_a, act_bh], axis=0)
    cold_in = jnp.concatenate([act_bc, act_l], axis=0)
    part = iota((rows, 256), 0) % 16 // 4
    spill = [jnp.zeros((rows, 256), F32)] * 2
    for i in range(GROUPS):
        q = i // 2
        lanes = slice(256 * (i % 2), 256 * (i % 2) + 256)
        oh = nt(hot_in, rows_of(wd_ref, hot, i))
        oc = nt(cold_in, rows_of(wd_ref, cold, i))
        out_ref[src, MAIN * q : MAIN * q + 16, lanes] = oh[:rows].astype(BF16).reshape(n, 16, 256)
        out_ref[src, MAIN * q + 16 : MAIN * q + 32, lanes] = (oh[rows:] + oc[:rows]).astype(BF16).reshape(n, 16, 256)
        spill[i % 2] = jnp.where(part == q, oc[rows:], spill[i % 2])
    out_ref[src, MAIN * QUARTERS :, :] = jnp.concatenate(spill, axis=1).astype(BF16).reshape(n, 16, QW)


def layer_kernel(
    spare_ref, skip_ref, resid_ref, gate_in_ref, gate_kern_ref, value_kern_ref, filt_ref, gain_ref, idst_ref, wtst_ref,
    row_ref, wg_hbm, wu_hbm, wd_hbm, out_ref,
    vsend, vrecv, fsend, frecv, csend, crecv, tail_send, tail_recv, rim_ref, wide_ref, hrow_ref, x_ref, bank_ref, acc_ref,
    hid_ref, normed_ref, slott_ref, slot_ref, weight_ref, sel_ref, left_ref, wmain_ref, wleft_ref,
    send, recv, give, ret, ssend, srecv, wg_ref, wu_ref, wd_ref,
    b_sem, w_sem, t_ssem, t_rsem, f_ssem, f_rsem, v_ssem, v_rsem, c_ssem, c_rsem, s_ssem, s_rsem, d_ssem, d_rsem, r_ssem, r_rsem,
):
    e, z = lax.axis_index("expert"), lax.axis_index("seq")

    sub, side = e // 8 * 4 + e % 4, e // 4 % 2

    def device(order, sign=1):
        return ahead(e, partner(order), sign)

    def remote(source, sink, ssem, rsem, expert, seq):
        pltpu.make_async_remote_copy(
            src_ref=source, dst_ref=sink, send_sem=ssem, recv_sem=rsem, device_id=(expert, seq), device_id_type=MESH
        ).start()

    def await_bytes(ref, sem):
        pltpu.make_async_copy(ref, ref, sem).wait()

    barrier = pltpu.get_barrier_semaphore()
    before = ((e + HOMES - 1 + (z + GROUPS - 1) // GROUPS) % HOMES, (z + GROUPS - 1) % GROUPS)
    after = ((e + (z + 1) // GROUPS) % HOMES, (z + 1) % GROUPS)
    pl.semaphore_signal(barrier, inc=1, device_id=before, device_id_type=MESH)

    def greet_line(dz, _):
        pl.semaphore_signal(barrier, inc=1, device_id=(e, (z + dz) % GROUPS), device_id_type=MESH)
        return 0

    def greet_plane(order, _):
        pl.semaphore_signal(barrier, inc=1, device_id=(device(order), z), device_id_type=MESH)
        return 0

    lax.fori_loop(1, GROUPS, greet_line, 0)
    lax.fori_loop(0, HOMES - 1, greet_plane, 0)
    weights = [
        pltpu.make_async_copy(hbm, vmem, w_sem.at[i])
        for i, (hbm, vmem) in enumerate(((wg_hbm, wg_ref), (wu_hbm, wu_ref), (wd_hbm, wd_ref)))
    ]
    for copy in weights:
        copy.start()
    ident = eye(256)
    flipped = nt(ident, filt_ref[...]).reshape(HALVES, SUBS, CH, 128)
    for h in range(HALVES):
        fsend[:, h] = flipped[h]
    tail = jnp.concatenate(
        [ref[TOK - 16 :, :].astype(F32)[14:16] for ref in (gate_in_ref, resid_ref)], axis=0
    )
    tail_send[...] = jnp.concatenate([tail[:, QW * q : QW * q + QW] for q in range(QUARTERS)], axis=0).astype(BF16)
    pl.semaphore_wait(barrier, GROUPS - 1 + HOMES - 1 + 1)

    remote(tail_send, tail_recv, t_ssem, t_rsem, *after)

    def greet_again(dz, _):
        pl.semaphore_signal(b_sem, inc=1, device_id=(e, (z + dz) % GROUPS), device_id_type=MESH)
        return 0

    lax.fori_loop(1, GROUPS, greet_again, 0)

    def send_filter(order, _):
        target = device(order)
        remote(fsend.at[target // 8 * 4 + target % 4], frecv.at[e], f_ssem, f_rsem, target, z)
        return 0

    lax.fori_loop(0, HOMES - 1, send_filter, 0)
    frecv[e] = fsend[sub]
    at_start = (z == 0) & (e % 2 == 0)

    def branch(ref, which, cols, kernel):
        return short_conv(
            ref[:, cols].astype(F32), rim_ref[2 * which : 2 * which + 1, cols], rim_ref[2 * which + 1 : 2 * which + 2, cols], kernel
        )

    def mate(t):
        target = (e // 8 + t // 4) % 4 * 8 + side * 4 + (e // 2 + t // 2) % 2 * 2 + (e + t) % 2
        return target, target // 8 * 4 + target % 4

    def place_of(expert, seq):
        return (expert % 2 * GROUPS + seq) * (SEQS // HALVES) + expert // 8 * 2 + expert // 2 % 2

    await_bytes(tail_recv, t_rsem)
    tail = tail_recv[...].astype(F32)
    for q in range(QUARTERS):
        rim_ref[:, QW * q : QW * q + QW] = jnp.where(at_start, 0.0, tail[4 * q : 4 * q + 4])
    row = place_of(e, z)

    def send_values(h, there):
        def one(t, _):
            target, share = mate(t)
            remote(vsend.at[there, h * SUBS + share], vrecv.at[h, row], v_ssem, v_rsem.at[h], target, there)
            return 0

        lax.fori_loop(1, SUBS, one, 0)

        @pl.when(there != z)
        def _():
            remote(vsend.at[there, h * SUBS + sub], vrecv.at[h, row], v_ssem, v_rsem.at[h], e, there)

    def make_values(r, _):
        there = (z + 3 * r + 4) % GROUPS
        cols = group_cols(there)
        values = branch(resid_ref, 1, cols, value_kern_ref[:, cols]).astype(BF16)
        vsend[there] = to_message(nt(ident, values))

        @pl.when(r == 0)
        def _():
            pl.semaphore_wait(b_sem, GROUPS - 1)

        send_values(0, there)
        return 0

    lax.fori_loop(0, GROUPS, make_values, 0)

    def rest_of_values(r, _):
        send_values(1, (z + 3 * r + 4) % GROUPS)
        return 0

    lax.fori_loop(0, GROUPS, rest_of_values, 0)
    for h in range(HALVES):
        vrecv[h, row] = vsend[z, h * SUBS + sub]

    await_bytes(frecv.at[pl.ds(0, HOMES - 1)], f_rsem)
    for d in range(HOMES):
        for h in range(HALVES):
            hrow_ref[CH * h : CH * h + CH, 128 * d : 128 * d + 128] = frecv[d, h]
    bank_ref[:, :, :PAD] = jnp.zeros((CH, 128, PAD), BF16)

    def make_bank(h):
        def bank(c, _):
            build_bank(hrow_ref[pl.ds(CH * h + c, 1), :], bank_ref.at[c])
            return 0

        lax.fori_loop(0, CH, bank, 0)

    make_bank(0)
    prepare_routing(row_ref, idst_ref, wtst_ref, slott_ref, slot_ref, weight_ref)

    def select(g, _):
        sel = []
        left = []
        for j in range(PER):
            home = device(PER * g + j)
            even = slott_ref[pl.ds(2 * home, 1), :]
            odd = slott_ref[pl.ds(2 * home + 1, 1), :]
            r = iota((MAIN, TOK), 0).astype(F32)
            sel.append(((even == r) | (odd == r)).astype(BF16))
            r = (iota((16, TOK), 0) % 4 + MAIN).astype(F32)
            left.append(((even == r) | (odd == r)).astype(BF16))
        sel_ref[g] = jnp.concatenate(sel, axis=0)
        left_ref[g] = jnp.concatenate(left, axis=0)
        want = (iota((TOK, PER * MAIN), 1) % MAIN).astype(F32)
        wmain_ref[g, 0], wmain_ref[g, 1] = part_weights(e, g, MAIN, want, slot_ref, weight_ref)
        want = (iota((TOK, PER * 16), 1) % 4 + MAIN).astype(F32)
        wleft_ref[g, 0], wleft_ref[g, 1] = part_weights(e, g, 16, want, slot_ref, weight_ref)
        return 0

    lax.fori_loop(0, PARTS, select, 0)
    def convolve(h):
        await_bytes(vrecv.at[h, pl.ds(0, NEAR - 1)], v_rsem.at[h])
        for i in range(8):
            wide_ref[256 * i : 256 * i + 256] = vrecv[h, 16 * i : 16 * i + 16].astype(F32).reshape(256, 128)
        for c in range(CH):
            for half in range(2):
                x_ref[c, :, 128 * half : 128 * half + 128] = wide_ref[pl.ds(8 * half + c, ROWS, stride=16), :]

        def conv(c, _):
            acc_ref[...] = x_ref[c] * skip_ref[h * SUBS * CH + sub * CH + c]
            for k in range(BLOCKS):
                upper = bank_ref[c, :, PAD + 256 * k : PAD + 256 * k + 256]
                lower = bank_ref[c, :, 256 * k : 256 * k + 256]
                lhs = x_ref[c, : ROWS - 8 * k, :].astype(BF16)
                acc_ref[8 * k :, :] += mm(lhs, jnp.concatenate([upper, lower], axis=0))
            x_ref[c] = acc_ref[...]
            return 0

        lax.fori_loop(0, CH, conv, 0)
        for c in range(CH):
            for half in range(2):
                wide_ref[pl.ds(8 * half + c, ROWS, stride=16), :] = x_ref[c, :, 128 * half : 128 * half + 128]
        for i in range(8):
            csend[h, 16 * i : 16 * i + 16] = wide_ref[256 * i : 256 * i + 256].reshape(16, 16, 128).astype(BF16)

        def send_back(i, _):
            there = (z + arrival(i)) % GROUPS
            sem = c_rsem.at[h * GROUPS + i]

            def send_plane(t, _):
                target, _ = mate(t)
                remote(csend.at[h, place_of(target, there)], crecv.at[h, i, sub], c_ssem, sem, target, there)
                return 0

            lax.fori_loop(1, SUBS, send_plane, 0)

            @pl.when(there != z)
            def _():
                remote(csend.at[h, place_of(e, there)], crecv.at[h, i, sub], c_ssem, sem, e, there)

            return 0

        lax.fori_loop(0, GROUPS, send_back, 0)
        pltpu.make_async_copy(csend.at[h, row], crecv.at[h, 0, sub], c_rsem.at[h * GROUPS]).start()

    convolve(0)
    make_bank(1)

    def piece_cols(p):
        group = (z + GROUPS - arrival(p % GROUPS)) % GROUPS
        return pl.ds(pl.multiple_of(group * 256 + p // GROUPS * 128, 128), 128)

    def rows_of(ref, which, i):
        return jnp.concatenate([ref[which, piece_cols(jnp.int32(p)), :] for p in (2 * i, 2 * i + 1)], axis=0)

    def take(p, total):
        h, i = p // GROUPS, p % GROUPS
        await_bytes(crecv.at[h, i], c_rsem.at[p])
        cols, mine = piece_cols(p), pl.ds(pl.multiple_of(128 * p, 128), 128)
        gated = branch(gate_in_ref, 0, cols, gate_kern_ref[:, cols])
        hidden = resid_ref[:, cols].astype(F32) + gated * from_message(crecv[h, i])
        hid_ref[:, mine] = hidden
        normed_ref[:, mine] = (hidden * gain_ref[:, cols]).astype(BF16)
        return total + jnp.sum(hidden * hidden, axis=1, keepdims=True)

    def take_quarter(q, total):
        return lax.fori_loop(4 * q, 4 * q + 4, take, total)

    def main_rows(q, g):
        cols = pl.ds(pl.multiple_of(QW * q, QW), QW)
        block = mm(sel_ref[g], normed_ref[:, cols]).astype(BF16).reshape(PER, MAIN, QW)
        send[pl.ds(PER * g, PER), pl.ds(pl.multiple_of(MAIN * q, MAIN), MAIN), :] = block

    def each_partner(g, action):
        for j in range(PER):
            order = PER * g + (j + e) % PER

            @pl.when(order != HOMES - 1)
            def _():
                action(order)

    def dispatch_early(q, total):
        total = take_quarter(q, total)

        def one_part(g, _):
            main_rows(q, g)
            rows = pl.ds(pl.multiple_of(MAIN * q, MAIN), MAIN)
            each_partner(
                g, lambda o: remote(send.at[o, rows], recv.at[o, rows], d_ssem, d_rsem.at[g], device(o), z)
            )
            return 0

        lax.fori_loop(0, PARTS, one_part, 0)
        return total

    total = dispatch_early(jnp.int32(0), jnp.zeros((TOK, 1), F32))
    convolve(1)
    total = lax.fori_loop(1, QUARTERS - 1, dispatch_early, total)
    total = take_quarter(QUARTERS - 1, total)
    scale = lax.rsqrt(total * (1.0 / WIDTH) + 1e-05)

    def dispatch_last(g, _):
        main_rows(QUARTERS - 1, g)
        part = iota((16 * PER, TOK), 0) % 16 // 4
        spill = jnp.zeros((16 * PER, QW), F32)
        wide = left_ref[g].astype(F32)
        for q in range(QUARTERS):
            spill += mm(jnp.where(part == q, wide, 0.0).astype(BF16), normed_ref[:, QW * q : QW * q + QW])
        send[pl.ds(PER * g, PER), MAIN * QUARTERS :, :] = spill.astype(BF16).reshape(PER, 16, QW)
        lines = []
        for per in (MAIN, 16):
            want = iota((TOK, PER * per), 1) % (MAIN if per == MAIN else 4) + (0 if per == MAIN else MAIN)
            hit = part_hits(e, g, per, want.astype(F32), slot_ref)
            lines.append(jnp.sum(jnp.where(hit[0] | hit[1], scale, 0.0), axis=0, keepdims=True))
        ssend[g] = jnp.concatenate(
            [lines[0][:, :128], lines[0][:, 128:], lines[1], jnp.zeros((5, 128), F32)], axis=0
        )
        rows = pl.ds(MAIN * (QUARTERS - 1), MAIN + 16)

        def action(o):
            remote(send.at[o, rows], recv.at[o, rows], d_ssem, d_rsem.at[g], device(o), z)
            remote(ssend.at[g], srecv.at[o], s_ssem, s_rsem.at[g], device(o), z)

        each_partner(g, action)

        @pl.when(g == PARTS - 1)
        def _():
            pltpu.make_async_copy(send.at[HOMES - 1], recv.at[HOMES - 1], d_rsem.at[g]).start()
            pltpu.make_async_copy(ssend.at[g], srecv.at[HOMES - 1], s_rsem.at[g]).start()

        return 0

    lax.fori_loop(0, PARTS, dispatch_last, 0)
    for copy in weights:
        copy.wait()
    hot = spare_ref[(e + 16) % 32]

    def expert(g, _):
        await_bytes(recv.at[pl.ds(PER * g, PER)], d_rsem.at[g])
        await_bytes(srecv.at[pl.ds(PER * g, PER)], s_rsem.at[g])
        ffn_group(g, rows_of, srecv, recv, wg_ref, wu_ref, wd_ref, give, hot)
        for part in range(3):
            rows = pl.ds(48 * part, 48)
            each_partner(g, lambda o: remote(give.at[o, rows], ret.at[o, rows], r_ssem, r_rsem.at[g], device(o, -1), z))

        @pl.when(g == PARTS - 1)
        def _():
            pltpu.make_async_copy(give.at[HOMES - 1], ret.at[HOMES - 1], r_rsem.at[g]).start()

        return 0

    lax.fori_loop(0, PARTS, expert, 0)

    def combine(g, _):
        await_bytes(ret.at[pl.ds(PER * g, PER)], r_rsem.at[g])
        left = ret[pl.ds(PER * g, PER), MAIN * QUARTERS :, :].reshape(PER * 16, QW)
        part = iota((TOK, PER * 16), 1) % 16 // 4
        for q in range(QUARTERS):
            main = ret[pl.ds(PER * g, PER), MAIN * q : MAIN * q + MAIN, :].reshape(PER * MAIN, QW)
            moe = mm(wmain_ref[g, 0], main) + mm(wmain_ref[g, 1], main)
            for w in range(2):
                moe += mm(jnp.where(part == q, wleft_ref[g, w].astype(F32), 0.0).astype(BF16), left)
            cut = slice(QW * q, QW * q + QW)
            hid_ref[:, cut] += moe
        return 0

    lax.fori_loop(0, PARTS, combine, 0)
    for p in range(PIECES):
        out_ref[:, piece_cols(jnp.int32(p))] = hid_ref[:, 128 * p : 128 * p + 128].astype(BF16)
    await_bytes(tail_send, t_ssem)
    await_bytes(frecv.at[pl.ds(0, HOMES - 1)], f_ssem)
    for sem in (v_ssem, c_ssem):
        await_bytes(csend.at[:, pl.ds(0, NEAR - 1)], sem)
    await_bytes(srecv.at[pl.ds(0, HOMES - 1)], s_ssem)
    await_bytes(send.at[pl.ds(0, HOMES - 1)], d_ssem)
    await_bytes(send.at[pl.ds(0, HOMES - 1)], r_ssem)


def body(
    resid,
    gate_in,
    gate_short,
    value_short,
    long_filter,
    skip_gain,
    norm_gain,
    expert_ids,
    gate_wts,
    spare_pick,
    w_gate,
    w_up,
    w_down,
):
    vmem, smem, anywhere = (pl.BlockSpec(memory_space=space) for space in (pltpu.VMEM, pltpu.SMEM, pl.ANY))
    dma = pltpu.SemaphoreType.DMA
    message = pltpu.VMEM((HOMES, MSG, QW), BF16)
    by_row = pltpu.VMEM((HALVES, NEAR, 16, 128), BF16)
    scratch = [
        pltpu.VMEM((GROUPS, HOMES, 16, 128), BF16),
        by_row,
        pltpu.VMEM((SUBS, HALVES, CH, 128), F32),
        pltpu.VMEM((HOMES, HALVES, CH, 128), F32),
        by_row,
        pltpu.VMEM((HALVES, GROUPS, SUBS, 16, 128), BF16),
        pltpu.VMEM((16, QW), BF16),
        pltpu.VMEM((16, QW), BF16),
        pltpu.VMEM((4, WIDTH), F32),
        pltpu.VMEM((ROWS * 16, 128), F32),
        pltpu.VMEM((HALVES * CH, POS), F32),
        pltpu.VMEM((CH, ROWS, 256), F32),
        pltpu.VMEM((CH, 128, PAD + POS), BF16),
        pltpu.VMEM((ROWS, 256), F32),
        pltpu.VMEM((TOK, WIDTH), F32),
        pltpu.VMEM((TOK, WIDTH), BF16),
        pltpu.VMEM((64, TOK), F32),
        pltpu.VMEM((TOK, 64), BF16),
        pltpu.VMEM((2, TOK, 64), BF16),
        pltpu.VMEM((PARTS, PER * MAIN, TOK), BF16),
        pltpu.VMEM((PARTS, PER * 16, TOK), BF16),
        pltpu.VMEM((PARTS, 2, TOK, PER * MAIN), BF16),
        pltpu.VMEM((PARTS, 2, TOK, PER * 16), BF16),
        message,
        message,
        message,
        message,
        pltpu.VMEM((PARTS, 8, 128), F32),
        pltpu.VMEM((HOMES, 8, 128), F32),
        pltpu.VMEM(w_gate.shape, BF16),
        pltpu.VMEM(w_up.shape, BF16),
        pltpu.VMEM(w_down.shape, BF16),
        pltpu.SemaphoreType.REGULAR,
        dma((3,)),
        dma,
        dma,
        dma,
        dma,
        dma,
        dma((HALVES,)),
        dma,
        dma((PIECES,)),
        dma,
        dma((PARTS,)),
        dma,
        dma((PARTS,)),
        dma,
        dma((PARTS,)),
    ]
    return pl.pallas_call(
        layer_kernel,
        out_shape=jax.ShapeDtypeStruct((TOK, WIDTH), BF16),
        in_specs=[smem] * 2 + [vmem] * 9 + [anywhere] * 3,
        out_specs=vmem,
        scratch_shapes=scratch,
        compiler_params=pltpu.CompilerParams(vmem_limit_bytes=VMEM_LIMIT, collective_id=0, has_side_effects=True),
        name="layer",
    )(
        spare_pick,
        skip_gain,
        resid,
        gate_in,
        gate_short,
        value_short,
        long_filter,
        norm_gain.reshape(1, WIDTH),
        expert_ids.T,
        gate_wts.T,
        spare_pick.reshape(1, HOMES),
        w_gate,
        w_up,
        w_down,
    )


def solution(mesh):
    placed = (
        P(("expert", "seq"), None),
        P(("expert", "seq"), None),
        P(),
        P(),
        P("expert", "seq"),
        P("seq"),
        P(),
        P(("expert", "seq"), None),
        P(("expert", "seq"), None),
        P(),
        P("expert", None, None),
        P("expert", None, None),
        P("expert", None, None),
    )
    return jax.shard_map(
        body, mesh=mesh, in_specs=placed, out_specs=P(("expert", "seq"), None), check_vma=False
    )
```

```python
import functools

import jax
import jax.numpy as jnp
from jax import lax
from jax.experimental import pallas as pl
from jax.experimental.pallas import tpu as pltpu
from jax.sharding import PartitionSpec as P

F32, BF16, I32 = jnp.float32, jnp.bfloat16, jnp.int32
VMEM_LIMIT = 60 * 1024 * 1024
TOK = 256
WIDTH = 2048
HOMES = 32
GROUPS = 8
SEQS = 16
BLOCKS = 16
CH = 8
HALVES = 2
SUBS = 16
ROWS = SEQS // HALVES * BLOCKS
PIECES = HALVES * GROUPS
POS = SEQS * TOK
QUARTERS = 4
QW = WIDTH // QUARTERS
MAIN = 32
LEFT = 4
MSG = QUARTERS * (MAIN + LEFT)
CAP = 12
HID = 256
PAD = 128
NEAR = SUBS * GROUPS
PARTS = 4
PER = HOMES // PARTS
MESH = pl.DeviceIdType.MESH


def iota(shape, dim):
    return lax.broadcasted_iota(I32, shape, dim)


def eye(n):
    return (iota((n, n), 0) == iota((n, n), 1)).astype(BF16)


def nt(a, b):
    return lax.dot_general(a, b, (((1,), (1,)), ((), ())), preferred_element_type=F32)


def mm(a, b):
    return jnp.dot(a, b, preferred_element_type=F32)


def short_conv(x, before2, before1, kernel):
    row = iota(x.shape, 0)
    back1 = jnp.where(row == 0, before1, pltpu.roll(x, 1, 0))
    back2 = jnp.where(row == 0, before2, jnp.where(row == 1, before1, pltpu.roll(x, 2, 0)))
    return kernel[0:1] * x + kernel[1:2] * back1 + kernel[2:3] * back2


def group_cols(g):
    return pl.ds(pl.multiple_of(g * 256, 256), 256)


def to_message(block):
    first = block[:, :128].reshape(32, 8, 128)
    second = block[:, 128:].reshape(32, 8, 128)
    return jnp.concatenate([first, second], axis=1).astype(BF16)


def from_message(message):
    wide = message.astype(F32)
    first = wide[:, :8].reshape(128, 128).astype(BF16)
    second = wide[:, 8:].reshape(128, 128).astype(BF16)
    ident = eye(128)
    return jnp.concatenate([nt(ident, first), nt(ident, second)], axis=0)


def partner(order):
    t = (order + 1) * 15 % 32
    return 2 * (t % 2) + t // 2 % 2, 2 * (t // 16) + t // 4 % 2, t // 8 % 2


def ahead(e, offset, sign):
    dx, dy, dc = offset
    x = (e // 8 + 4 + sign * dx) % 4
    y = (e // 2 % 4 + 4 + sign * dy) % 4
    return 8 * x + 2 * y + (e + dc) % 2


def slots(named, rep, axis):
    tri = (iota((TOK, TOK), axis) < iota((TOK, TOK), 1 - axis)).astype(BF16)
    if axis == 0:
        rank = mm(named.astype(BF16), tri)
    else:
        rank = mm(tri, named.astype(BF16))
    kept = (named > 0) & ((rank < CAP) | ((rank < 2 * CAP) & (rep > 0)))
    return jnp.where(kept, jnp.where(rep > 0, rank, rank + 2 * CAP), -1.0)


def prepare_routing(spare_ref, idst_ref, wtst_ref, slott_ref, slot_ref, weight_ref):
    expert, index = iota((64, HOMES), 0), iota((64, HOMES), 1)
    picked = jnp.where(index == (expert // 2 + 16) % 32, spare_ref[...], 0)
    rep = jnp.sum(picked.astype(F32), axis=1, keepdims=True) == (iota((64, 1), 0) % 2).astype(F32)
    named = jnp.zeros((64, TOK), F32)
    weight = jnp.zeros((64, TOK), F32)
    for k in range(4):
        hit = idst_ref[k : k + 1, :] == iota((64, TOK), 0)
        named += hit.astype(F32)
        weight += jnp.where(hit, wtst_ref[k : k + 1, :], 0.0)
    slot = slots(named, rep.astype(F32), 0)
    slott_ref[...] = slot
    ident = eye(TOK)
    slot_ref[...] = nt(ident, slot.astype(BF16)).astype(BF16)
    high = weight.astype(BF16)
    weight_ref[0] = nt(ident, high).astype(BF16)
    weight_ref[1] = nt(ident, (weight - high.astype(F32)).astype(BF16)).astype(BF16)


def part_picks(e, g, per):
    shape = (64, PER * per)
    home = ahead(e, partner(PER * g + iota(shape, 1) // per), 1)
    return [(iota(shape, 0) == 2 * home + odd).astype(BF16) for odd in range(2)]


def part_hits(e, g, per, want, slot_ref):
    return [mm(slot_ref[...], pick) == want for pick in part_picks(e, g, per)]


def part_weights(e, g, per, want, slot_ref, weight_ref):
    high = low = jnp.zeros((TOK, PER * per), F32)
    for pick in part_picks(e, g, per):
        hit = mm(slot_ref[...], pick) == want
        high = high + jnp.where(hit, mm(weight_ref[0], pick), 0.0)
        low = low + jnp.where(hit, mm(weight_ref[1], pick), 0.0)
    return high.astype(BF16), low.astype(BF16)


def build_bank(row, bank_ref):
    wide = jnp.concatenate([jnp.broadcast_to(row, (8, POS)), jnp.zeros((8, PAD), F32)], axis=1)
    base = pltpu.roll(wide, 0, 1, stride=1, stride_axis=0)
    for a in range(8):
        upper = pltpu.roll(base, 16 * a, 1) if a else base
        lower = pltpu.roll(base, 16 * a + 8, 1)
        both = jnp.concatenate([upper, lower], axis=0)[:, :POS].astype(BF16)
        bank_ref[16 * a : 16 * a + 16, PAD:] = both


def arrival(i):
    return jnp.where(i % 2 == 1, (i + 1) // 2, GROUPS - i // 2) % GROUPS


def silu_mul(gate, up):
    return gate / (1.0 + jnp.exp(-gate)) * up


def scale_columns(g, scales, lanes_of, per):
    cols = []
    for j in range(PER):
        sub, lane, rows = lanes_of(j)
        line = scales[PER * g + j, sub : sub + 1, :]
        hit = iota((per, 128), 1) == lane + iota((per, 128), 0)
        cols.append(jnp.sum(jnp.where(hit, line, 0.0), axis=1, keepdims=True))
    return jnp.concatenate(cols, axis=0)


def ffn_group(g, rows_of, scales, recv_ref, wg_ref, wu_ref, wd_ref, out_ref, hot):
    cold = 1 - hot
    n = PER
    src = pl.ds(g * PER, n)
    rows = 16 * n
    zero = functools.partial(jnp.zeros, (rows, HID), F32)
    ga, ua, gb, ub, gc, uc, gl, ul = (zero() for _ in range(8))
    part = iota((rows, HID), 0) % 16 // 4
    for i in range(GROUPS):
        q = i // 2
        lanes = slice(256 * (i % 2), 256 * (i % 2) + 256)
        xa = recv_ref[src, MAIN * q : MAIN * q + 16, lanes].reshape(rows, 256)
        xb = recv_ref[src, MAIN * q + 16 : MAIN * q + 32, lanes].reshape(rows, 256)
        left = recv_ref[src, MAIN * QUARTERS :, lanes].reshape(rows, 256)
        both = jnp.concatenate([xa, xb], axis=0)
        gh, uh = mm(both, rows_of(wg_ref, hot, i)), mm(both, rows_of(wu_ref, hot, i))
        ga, ua, gb, ub = ga + gh[:rows], ua + uh[:rows], gb + gh[rows:], ub + uh[rows:]
        both = jnp.concatenate([xb, left], axis=0)
        gh, uh = mm(both, rows_of(wg_ref, cold, i)), mm(both, rows_of(wu_ref, cold, i))
        gc, uc = gc + gh[:rows], uc + uh[:rows]
        gl = gl + jnp.where(part == q, gh[rows:], 0.0)
        ul = ul + jnp.where(part == q, uh[rows:], 0.0)

    def over_quarters(acc):
        acc = acc.reshape(n, 16, HID)
        acc = acc[:, :8] + acc[:, 8:]
        acc = acc.reshape(8 * n, HID)
        low = iota(acc.shape, 0) % 8 < 4
        other = jnp.where(low, pltpu.roll(acc, 8 * n - 4, 0), pltpu.roll(acc, 4, 0))
        acc = (acc + other).reshape(n, 8, HID)
        return jnp.concatenate([acc, acc], axis=1).reshape(rows, HID)

    sa = scale_columns(g, scales, lambda j: (j // 4, 32 * (j % 4), 16), 16)
    sb = scale_columns(g, scales, lambda j: (j // 4, 32 * (j % 4) + 16, 16), 16)
    sl = scale_columns(g, scales, lambda j: (2, 16 * j, 16), 16)
    is_hot = iota((rows, HID), 0) % 16 < 8
    act_a = silu_mul(ga * sa, ua * sa).astype(BF16)
    act_b = silu_mul(jnp.where(is_hot, gb, gc) * sb, jnp.where(is_hot, ub, uc) * sb)
    act_bh = jnp.where(is_hot, act_b, 0.0).astype(BF16)
    act_bc = jnp.where(is_hot, 0.0, act_b).astype(BF16)
    act_l = silu_mul(over_quarters(gl) * sl, over_quarters(ul) * sl).astype(BF16)
    hot_in = jnp.concatenate([act_a, act_bh], axis=0)
    cold_in = jnp.concatenate([act_bc, act_l], axis=0)
    part = iota((rows, 256), 0) % 16 // 4
    spill = [jnp.zeros((rows, 256), F32)] * 2
    for i in range(GROUPS):
        q = i // 2
        lanes = slice(256 * (i % 2), 256 * (i % 2) + 256)
        oh = nt(hot_in, rows_of(wd_ref, hot, i))
        oc = nt(cold_in, rows_of(wd_ref, cold, i))
        out_ref[src, MAIN * q : MAIN * q + 16, lanes] = oh[:rows].astype(BF16).reshape(n, 16, 256)
        out_ref[src, MAIN * q + 16 : MAIN * q + 32, lanes] = (oh[rows:] + oc[:rows]).astype(BF16).reshape(n, 16, 256)
        spill[i % 2] = jnp.where(part == q, oc[rows:], spill[i % 2])
    out_ref[src, MAIN * QUARTERS :, :] = jnp.concatenate(spill, axis=1).astype(BF16).reshape(n, 16, QW)


def layer_kernel(
    spare_ref, skip_ref, resid_ref, gate_in_ref, gate_kern_ref, value_kern_ref, filt_ref, gain_ref, idst_ref, wtst_ref,
    row_ref, wg_hbm, wu_hbm, wd_hbm, out_ref,
    vsend, vrecv, fsend, frecv, csend, crecv, tail_send, tail_recv, rim_ref, wide_ref, hrow_ref, x_ref, bank_ref, acc_ref,
    hid_ref, normed_ref, slott_ref, slot_ref, weight_ref, sel_ref, left_ref, wmain_ref, wleft_ref,
    send, recv, give, ret, ssend, srecv, wg_ref, wu_ref, wd_ref,
    b_sem, w_sem, t_ssem, t_rsem, f_ssem, f_rsem, v_ssem, v_rsem, c_ssem, c_rsem, s_ssem, s_rsem, d_ssem, d_rsem, r_ssem, r_rsem,
):
    e, z = lax.axis_index("expert"), lax.axis_index("seq")

    sub, side = e // 8 * 4 + e % 4, e // 4 % 2

    def device(order, sign=1):
        return ahead(e, partner(order), sign)

    def remote(source, sink, ssem, rsem, expert, seq):
        pltpu.make_async_remote_copy(
            src_ref=source, dst_ref=sink, send_sem=ssem, recv_sem=rsem, device_id=(expert, seq), device_id_type=MESH
        ).start()

    def await_bytes(ref, sem):
        pltpu.make_async_copy(ref, ref, sem).wait()

    barrier = pltpu.get_barrier_semaphore()
    before = ((e + HOMES - 1 + (z + GROUPS - 1) // GROUPS) % HOMES, (z + GROUPS - 1) % GROUPS)
    after = ((e + (z + 1) // GROUPS) % HOMES, (z + 1) % GROUPS)
    pl.semaphore_signal(barrier, inc=1, device_id=before, device_id_type=MESH)

    def greet_line(dz, _):
        pl.semaphore_signal(barrier, inc=1, device_id=(e, (z + dz) % GROUPS), device_id_type=MESH)
        return 0

    def greet_plane(order, _):
        pl.semaphore_signal(barrier, inc=1, device_id=(device(order), z), device_id_type=MESH)
        return 0

    lax.fori_loop(1, GROUPS, greet_line, 0)
    lax.fori_loop(0, HOMES - 1, greet_plane, 0)
    weights = [
        pltpu.make_async_copy(hbm, vmem, w_sem.at[i])
        for i, (hbm, vmem) in enumerate(((wg_hbm, wg_ref), (wu_hbm, wu_ref), (wd_hbm, wd_ref)))
    ]
    for copy in weights:
        copy.start()
    ident = eye(256)
    flipped = nt(ident, filt_ref[...]).reshape(HALVES, SUBS, CH, 128)
    for h in range(HALVES):
        fsend[:, h] = flipped[h]
    tail = jnp.concatenate(
        [ref[TOK - 16 :, :].astype(F32)[14:16] for ref in (gate_in_ref, resid_ref)], axis=0
    )
    tail_send[...] = jnp.concatenate([tail[:, QW * q : QW * q + QW] for q in range(QUARTERS)], axis=0).astype(BF16)
    pl.semaphore_wait(barrier, GROUPS - 1 + HOMES - 1 + 1)

    remote(tail_send, tail_recv, t_ssem, t_rsem, *after)

    def greet_again(dz, _):
        pl.semaphore_signal(b_sem, inc=1, device_id=(e, (z + dz) % GROUPS), device_id_type=MESH)
        return 0

    lax.fori_loop(1, GROUPS, greet_again, 0)

    def send_filter(order, _):
        target = device(order)
        remote(fsend.at[target // 8 * 4 + target % 4], frecv.at[e], f_ssem, f_rsem, target, z)
        return 0

    lax.fori_loop(0, HOMES - 1, send_filter, 0)
    frecv[e] = fsend[sub]
    at_start = (z == 0) & (e % 2 == 0)

    def branch(ref, which, cols, kernel):
        return short_conv(
            ref[:, cols].astype(F32), rim_ref[2 * which : 2 * which + 1, cols], rim_ref[2 * which + 1 : 2 * which + 2, cols], kernel
        )

    def mate(t):
        target = (e // 8 + t // 4) % 4 * 8 + side * 4 + (e // 2 + t // 2) % 2 * 2 + (e + t) % 2
        return target, target // 8 * 4 + target % 4

    def place_of(expert, seq):
        return (expert % 2 * GROUPS + seq) * (SEQS // HALVES) + expert // 8 * 2 + expert // 2 % 2

    await_bytes(tail_recv, t_rsem)
    tail = tail_recv[...].astype(F32)
    for q in range(QUARTERS):
        rim_ref[:, QW * q : QW * q + QW] = jnp.where(at_start, 0.0, tail[4 * q : 4 * q + 4])
    row = place_of(e, z)

    def send_values(h, there):
        def one(t, _):
            target, share = mate(t)
            remote(vsend.at[there, h * SUBS + share], vrecv.at[h, row], v_ssem, v_rsem.at[h], target, there)
            return 0

        lax.fori_loop(1, SUBS, one, 0)

        @pl.when(there != z)
        def _():
            remote(vsend.at[there, h * SUBS + sub], vrecv.at[h, row], v_ssem, v_rsem.at[h], e, there)

    def make_values(r, _):
        there = (z + 3 * r + 4) % GROUPS
        cols = group_cols(there)
        values = branch(resid_ref, 1, cols, value_kern_ref[:, cols]).astype(BF16)
        vsend[there] = to_message(nt(ident, values))

        @pl.when(r == 0)
        def _():
            pl.semaphore_wait(b_sem, GROUPS - 1)

        send_values(0, there)
        return 0

    lax.fori_loop(0, GROUPS, make_values, 0)

    def rest_of_values(r, _):
        send_values(1, (z + 3 * r + 4) % GROUPS)
        return 0

    lax.fori_loop(0, GROUPS, rest_of_values, 0)
    for h in range(HALVES):
        vrecv[h, row] = vsend[z, h * SUBS + sub]

    await_bytes(frecv.at[pl.ds(0, HOMES - 1)], f_rsem)
    for d in range(HOMES):
        for h in range(HALVES):
            hrow_ref[CH * h : CH * h + CH, 128 * d : 128 * d + 128] = frecv[d, h]
    bank_ref[:, :, :PAD] = jnp.zeros((CH, 128, PAD), BF16)

    def make_bank(h):
        def bank(c, _):
            build_bank(hrow_ref[pl.ds(CH * h + c, 1), :], bank_ref.at[c])
            return 0

        lax.fori_loop(0, CH, bank, 0)

    make_bank(0)
    prepare_routing(row_ref, idst_ref, wtst_ref, slott_ref, slot_ref, weight_ref)

    def select(g, _):
        sel = []
        left = []
        for j in range(PER):
            home = device(PER * g + j)
            even = slott_ref[pl.ds(2 * home, 1), :]
            odd = slott_ref[pl.ds(2 * home + 1, 1), :]
            r = iota((MAIN, TOK), 0).astype(F32)
            sel.append(((even == r) | (odd == r)).astype(BF16))
            r = (iota((16, TOK), 0) % 4 + MAIN).astype(F32)
            left.append(((even == r) | (odd == r)).astype(BF16))
        sel_ref[g] = jnp.concatenate(sel, axis=0)
        left_ref[g] = jnp.concatenate(left, axis=0)
        want = (iota((TOK, PER * MAIN), 1) % MAIN).astype(F32)
        wmain_ref[g, 0], wmain_ref[g, 1] = part_weights(e, g, MAIN, want, slot_ref, weight_ref)
        want = (iota((TOK, PER * 16), 1) % 4 + MAIN).astype(F32)
        wleft_ref[g, 0], wleft_ref[g, 1] = part_weights(e, g, 16, want, slot_ref, weight_ref)
        return 0

    lax.fori_loop(0, PARTS, select, 0)
    def convolve(h):
        await_bytes(vrecv.at[h, pl.ds(0, NEAR - 1)], v_rsem.at[h])
        for i in range(8):
            wide_ref[256 * i : 256 * i + 256] = vrecv[h, 16 * i : 16 * i + 16].astype(F32).reshape(256, 128)
        for c in range(CH):
            for half in range(2):
                x_ref[c, :, 128 * half : 128 * half + 128] = wide_ref[pl.ds(8 * half + c, ROWS, stride=16), :]

        def conv(c, _):
            acc_ref[...] = x_ref[c] * skip_ref[h * SUBS * CH + sub * CH + c]
            for k in range(BLOCKS):
                upper = bank_ref[c, :, PAD + 256 * k : PAD + 256 * k + 256]
                lower = bank_ref[c, :, 256 * k : 256 * k + 256]
                lhs = x_ref[c, : ROWS - 8 * k, :].astype(BF16)
                acc_ref[8 * k :, :] += mm(lhs, jnp.concatenate([upper, lower], axis=0))
            x_ref[c] = acc_ref[...]
            return 0

        lax.fori_loop(0, CH, conv, 0)
        for c in range(CH):
            for half in range(2):
                wide_ref[pl.ds(8 * half + c, ROWS, stride=16), :] = x_ref[c, :, 128 * half : 128 * half + 128]
        for i in range(8):
            csend[h, 16 * i : 16 * i + 16] = wide_ref[256 * i : 256 * i + 256].reshape(16, 16, 128).astype(BF16)

        def send_back(i, _):
            there = (z + arrival(i)) % GROUPS
            sem = c_rsem.at[h * GROUPS + i]

            def send_plane(t, _):
                target, _ = mate(t)
                remote(csend.at[h, place_of(target, there)], crecv.at[h, i, sub], c_ssem, sem, target, there)
                return 0

            lax.fori_loop(1, SUBS, send_plane, 0)

            @pl.when(there != z)
            def _():
                remote(csend.at[h, place_of(e, there)], crecv.at[h, i, sub], c_ssem, sem, e, there)

            return 0

        lax.fori_loop(0, GROUPS, send_back, 0)
        pltpu.make_async_copy(csend.at[h, row], crecv.at[h, 0, sub], c_rsem.at[h * GROUPS]).start()

    convolve(0)
    make_bank(1)

    def piece_cols(p):
        group = (z + GROUPS - arrival(p % GROUPS)) % GROUPS
        return pl.ds(pl.multiple_of(group * 256 + p // GROUPS * 128, 128), 128)

    def rows_of(ref, which, i):
        return jnp.concatenate([ref[which, piece_cols(jnp.int32(p)), :] for p in (2 * i, 2 * i + 1)], axis=0)

    def take(p, total):
        h, i = p // GROUPS, p % GROUPS
        await_bytes(crecv.at[h, i], c_rsem.at[p])
        cols, mine = piece_cols(p), pl.ds(pl.multiple_of(128 * p, 128), 128)
        gated = branch(gate_in_ref, 0, cols, gate_kern_ref[:, cols])
        hidden = resid_ref[:, cols].astype(F32) + gated * from_message(crecv[h, i])
        hid_ref[:, mine] = hidden
        normed_ref[:, mine] = (hidden * gain_ref[:, cols]).astype(BF16)
        return total + jnp.sum(hidden * hidden, axis=1, keepdims=True)

    def take_quarter(q, total):
        return lax.fori_loop(4 * q, 4 * q + 4, take, total)

    def main_rows(q, g):
        cols = pl.ds(pl.multiple_of(QW * q, QW), QW)
        block = mm(sel_ref[g], normed_ref[:, cols]).astype(BF16).reshape(PER, MAIN, QW)
        send[pl.ds(PER * g, PER), pl.ds(pl.multiple_of(MAIN * q, MAIN), MAIN), :] = block

    def each_partner(g, action):
        for j in range(PER):
            order = PER * g + (j + e) % PER

            @pl.when(order != HOMES - 1)
            def _():
                action(order)

    def dispatch_early(q, total):
        total = take_quarter(q, total)

        def one_part(g, _):
            main_rows(q, g)
            rows = pl.ds(pl.multiple_of(MAIN * q, MAIN), MAIN)
            each_partner(
                g, lambda o: remote(send.at[o, rows], recv.at[o, rows], d_ssem, d_rsem.at[g], device(o), z)
            )
            return 0

        lax.fori_loop(0, PARTS, one_part, 0)
        return total

    total = dispatch_early(jnp.int32(0), jnp.zeros((TOK, 1), F32))
    convolve(1)
    total = lax.fori_loop(1, QUARTERS - 1, dispatch_early, total)
    total = take_quarter(QUARTERS - 1, total)
    scale = lax.rsqrt(total * (1.0 / WIDTH) + 1e-05)

    def dispatch_last(g, _):
        main_rows(QUARTERS - 1, g)
        part = iota((16 * PER, TOK), 0) % 16 // 4
        spill = jnp.zeros((16 * PER, QW), F32)
        wide = left_ref[g].astype(F32)
        for q in range(QUARTERS):
            spill += mm(jnp.where(part == q, wide, 0.0).astype(BF16), normed_ref[:, QW * q : QW * q + QW])
        send[pl.ds(PER * g, PER), MAIN * QUARTERS :, :] = spill.astype(BF16).reshape(PER, 16, QW)
        lines = []
        for per in (MAIN, 16):
            want = iota((TOK, PER * per), 1) % (MAIN if per == MAIN else 4) + (0 if per == MAIN else MAIN)
            hit = part_hits(e, g, per, want.astype(F32), slot_ref)
            lines.append(jnp.sum(jnp.where(hit[0] | hit[1], scale, 0.0), axis=0, keepdims=True))
        ssend[g] = jnp.concatenate(
            [lines[0][:, :128], lines[0][:, 128:], lines[1], jnp.zeros((5, 128), F32)], axis=0
        )
        rows = pl.ds(MAIN * (QUARTERS - 1), MAIN + 16)

        def action(o):
            remote(send.at[o, rows], recv.at[o, rows], d_ssem, d_rsem.at[g], device(o), z)
            remote(ssend.at[g], srecv.at[o], s_ssem, s_rsem.at[g], device(o), z)

        each_partner(g, action)

        @pl.when(g == PARTS - 1)
        def _():
            pltpu.make_async_copy(send.at[HOMES - 1], recv.at[HOMES - 1], d_rsem.at[g]).start()
            pltpu.make_async_copy(ssend.at[g], srecv.at[HOMES - 1], s_rsem.at[g]).start()

        return 0

    lax.fori_loop(0, PARTS, dispatch_last, 0)
    for copy in weights:
        copy.wait()
    hot = spare_ref[(e + 16) % 32]

    def expert(g, _):
        await_bytes(recv.at[pl.ds(PER * g, PER)], d_rsem.at[g])
        await_bytes(srecv.at[pl.ds(PER * g, PER)], s_rsem.at[g])
        ffn_group(g, rows_of, srecv, recv, wg_ref, wu_ref, wd_ref, give, hot)
        for part in range(3):
            rows = pl.ds(48 * part, 48)
            each_partner(g, lambda o: remote(give.at[o, rows], ret.at[o, rows], r_ssem, r_rsem.at[g], device(o, -1), z))

        @pl.when(g == PARTS - 1)
        def _():
            pltpu.make_async_copy(give.at[HOMES - 1], ret.at[HOMES - 1], r_rsem.at[g]).start()

        return 0

    lax.fori_loop(0, PARTS, expert, 0)

    def combine(g, _):
        await_bytes(ret.at[pl.ds(PER * g, PER)], r_rsem.at[g])
        left = ret[pl.ds(PER * g, PER), MAIN * QUARTERS :, :].reshape(PER * 16, QW)
        part = iota((TOK, PER * 16), 1) % 16 // 4
        for q in range(QUARTERS):
            main = ret[pl.ds(PER * g, PER), MAIN * q : MAIN * q + MAIN, :].reshape(PER * MAIN, QW)
            moe = mm(wmain_ref[g, 0], main) + mm(wmain_ref[g, 1], main)
            for w in range(2):
                moe += mm(jnp.where(part == q, wleft_ref[g, w].astype(F32), 0.0).astype(BF16), left)
            cut = slice(QW * q, QW * q + QW)
            hid_ref[:, cut] += moe
        return 0

    lax.fori_loop(0, PARTS, combine, 0)
    for p in range(PIECES):
        out_ref[:, piece_cols(jnp.int32(p))] = hid_ref[:, 128 * p : 128 * p + 128].astype(BF16)
    await_bytes(tail_send, t_ssem)
    await_bytes(frecv.at[pl.ds(0, HOMES - 1)], f_ssem)
    for sem in (v_ssem, c_ssem):
        await_bytes(csend.at[:, pl.ds(0, NEAR - 1)], sem)
    await_bytes(srecv.at[pl.ds(0, HOMES - 1)], s_ssem)
    await_bytes(send.at[pl.ds(0, HOMES - 1)], d_ssem)
    await_bytes(send.at[pl.ds(0, HOMES - 1)], r_ssem)


def body(
    resid,
    gate_in,
    gate_short,
    value_short,
    long_filter,
    skip_gain,
    norm_gain,
    expert_ids,
    gate_wts,
    spare_pick,
    w_gate,
    w_up,
    w_down,
):
    vmem, smem, anywhere = (pl.BlockSpec(memory_space=space) for space in (pltpu.VMEM, pltpu.SMEM, pl.ANY))
    dma = pltpu.SemaphoreType.DMA
    message = pltpu.VMEM((HOMES, MSG, QW), BF16)
    by_row = pltpu.VMEM((HALVES, NEAR, 16, 128), BF16)
    scratch = [
        pltpu.VMEM((GROUPS, HOMES, 16, 128), BF16),
        by_row,
        pltpu.VMEM((SUBS, HALVES, CH, 128), F32),
        pltpu.VMEM((HOMES, HALVES, CH, 128), F32),
        by_row,
        pltpu.VMEM((HALVES, GROUPS, SUBS, 16, 128), BF16),
        pltpu.VMEM((16, QW), BF16),
        pltpu.VMEM((16, QW), BF16),
        pltpu.VMEM((4, WIDTH), F32),
        pltpu.VMEM((ROWS * 16, 128), F32),
        pltpu.VMEM((HALVES * CH, POS), F32),
        pltpu.VMEM((CH, ROWS, 256), F32),
        pltpu.VMEM((CH, 128, PAD + POS), BF16),
        pltpu.VMEM((ROWS, 256), F32),
        pltpu.VMEM((TOK, WIDTH), F32),
        pltpu.VMEM((TOK, WIDTH), BF16),
        pltpu.VMEM((64, TOK), F32),
        pltpu.VMEM((TOK, 64), BF16),
        pltpu.VMEM((2, TOK, 64), BF16),
        pltpu.VMEM((PARTS, PER * MAIN, TOK), BF16),
        pltpu.VMEM((PARTS, PER * 16, TOK), BF16),
        pltpu.VMEM((PARTS, 2, TOK, PER * MAIN), BF16),
        pltpu.VMEM((PARTS, 2, TOK, PER * 16), BF16),
        message,
        message,
        message,
        message,
        pltpu.VMEM((PARTS, 8, 128), F32),
        pltpu.VMEM((HOMES, 8, 128), F32),
        pltpu.VMEM(w_gate.shape, BF16),
        pltpu.VMEM(w_up.shape, BF16),
        pltpu.VMEM(w_down.shape, BF16),
        pltpu.SemaphoreType.REGULAR,
        dma((3,)),
        dma,
        dma,
        dma,
        dma,
        dma,
        dma((HALVES,)),
        dma,
        dma((PIECES,)),
        dma,
        dma((PARTS,)),
        dma,
        dma((PARTS,)),
        dma,
        dma((PARTS,)),
    ]
    return pl.pallas_call(
        layer_kernel,
        out_shape=pltpu.VMEM((TOK, WIDTH), BF16),
        in_specs=[smem] * 2 + [vmem] * 9 + [anywhere] * 3,
        out_specs=vmem,
        scratch_shapes=scratch,
        compiler_params=pltpu.CompilerParams(vmem_limit_bytes=VMEM_LIMIT, collective_id=0, has_side_effects=True),
        name="layer",
    )(
        spare_pick,
        skip_gain,
        resid,
        gate_in,
        gate_short,
        value_short,
        long_filter,
        norm_gain.reshape(1, WIDTH),
        expert_ids.T,
        gate_wts.T,
        spare_pick.reshape(1, HOMES),
        w_gate,
        w_up,
        w_down,
    )


def solution(mesh):
    placed = (
        P(("expert", "seq"), None),
        P(("expert", "seq"), None),
        P(),
        P(),
        P("expert", "seq"),
        P("seq"),
        P(),
        P(("expert", "seq"), None),
        P(("expert", "seq"), None),
        P(),
        P("expert", None, None),
        P("expert", None, None),
        P("expert", None, None),
    )
    return jax.shard_map(
        body, mesh=mesh, in_specs=placed, out_specs=P(("expert", "seq"), None), check_vma=False
    )
```
